256 devices in a mesh: lat: 64 (over z, y, core), ch: 4 (over x).
Axes of the slice: x: 4, y: 4, z: 8, core: 2. Of those that a mesh axis runs over, the one named last changes fastest.
Arguments:
- grid: bfloat16 [512, 1440, 512], P('lat', None, 'ch'), may hold values from -6 to 6
- legendre: bfloat16 [384, 384, 512], P('lat'), may hold values from -1 to 1, as said below
- m_order: int32 [384], replicated, may hold values from 0 to 383, as said below
- quad_weights: float32 [512], replicated, may hold values from 0.5 to 1.5
- mix_real: bfloat16 [512, 512], replicated, may hold values from -0.1875 to 0.1875
- mix_imag: bfloat16 [512, 512], replicated, may hold values from -0.1875 to 0.1875
- spec_gain: float32 [384, 512], replicated, may hold values from 0.5 to 2
- ln_gain: float32 [512], replicated, may hold values from 0.5 to 1.5
- mlp_in: bfloat16 [512, 1024], replicated, may hold values from -0.25 to 0.25
- mlp_bias: float32 [1024], replicated, may hold values from -3 to 3
- mlp_out: bfloat16 [1024, 512], replicated, may hold values from -0.1875 to 0.1875
Outputs:
- block_out: bfloat16 [512, 1440, 512], P('lat', 'ch')
The draws below stay inside these ranges and needn't reach their ends.
Inputs may be any that keep to these rules, and one draw needn't show every extreme that they name: `m_order`: a permutation of 0 to 383. legendre[r, l, cycle] is zero wherever l < m_order[r].
All inputs are finite; a program needn't handle non-finite values.
Results may differ from the reference program's by a relative error of at most 0.013.
Values may be sent and summed in bfloat16 or wider, within the bound.
A program may use at most 64 MiB of HBM per device.

```python
import math
import jax
import jax.numpy as jnp
from jax import lax

NLAT = 512
NLON = 1440
C = 512
H = 1024
MODES = 384


def order_helper(key):
    return jax.random.permutation(key, MODES).astype(jnp.int32)


def draw_m_order(key, part):
    return order_helper(key)


def draw_legendre(key, part):
    order = order_helper(key)
    key = jax.random.fold_in(key, 7)
    values = jax.random.truncated_normal(key, -4.0, 4.0, (MODES, MODES, NLAT), jnp.float32) * NLAT ** (-0.5)
    degree = jnp.arange(MODES, dtype=jnp.int32)
    keep = degree[None, :, None] >= order[:, None, None]
    return jnp.where(keep, values, 0.0).astype(jnp.bfloat16)


def shard_levels(own_key, extent, pieces, least, largest):
    def one(axis_at, blocks):
        draws = jax.random.uniform(jax.random.fold_in(jax.random.fold_in(own_key, 6), axis_at), (blocks,), jnp.float32, least / len(pieces), largest / len(pieces))
        return jnp.repeat(jnp.exp(draws), extent[axis_at] // blocks).reshape((-1,) + (1,) * (len(extent) - axis_at - 1))

    loudness = one(*pieces[0])
    for cut in pieces[1:]:
        loudness = loudness * one(*cut)
    return loudness


def noise(key, extent, width, bound, cuts=(), kind=jnp.bfloat16):
    level = shard_levels(key, extent, cuts, -0.22, 0.18) if cuts else 1.0
    result = jax.random.normal(key, extent, jnp.float32) * width * level
    return jnp.minimum(jnp.maximum(result, -bound), bound).astype(kind)


def setup_inputs(seed: int = 0) -> dict:
    streams_of = jax.random.split(jax.random.key(seed), 12)
    return {
        "grid": noise(streams_of[0], (NLAT, NLON, C), 1.0, 6.0, ((0, 64), (2, 4))),
        "legendre": draw_legendre(jax.random.fold_in(streams_of[11], 71), 0),
        "m_order": draw_m_order(jax.random.fold_in(streams_of[11], 71), 0),
        "quad_weights": jnp.clip(jax.random.uniform(streams_of[3], (NLAT,), jnp.float32, 0.5, 1.5), 0.5, 1.5),
        "mix_real": noise(streams_of[4], (C, C), (2 * C) ** -0.5, 0.1875),
        "mix_imag": noise(streams_of[5], (C, C), (2 * C) ** -0.5, 0.1875),
        "spec_gain": jnp.clip(jnp.exp(jax.random.uniform(streams_of[6], (MODES, C), jnp.float32, math.log(0.5), math.log(2.0))), 0.5, 2.0),
        "ln_gain": jnp.clip(1.0 + 0.1 * jax.random.normal(streams_of[7], (C,), jnp.float32), 0.5, 1.5),
        "mlp_in": noise(streams_of[8], (C, H), C ** -0.5, 0.25),
        "mlp_bias": noise(streams_of[9], (H,), 0.5, 3.0, (), jnp.float32),
        "mlp_out": noise(streams_of[10], (H, C), H ** -0.5, 0.1875),
    }


def forward_tables(order, nlon):
    steps = jnp.arange(nlon, dtype=jnp.int32)
    index = steps[:, None] * order[None, :] % nlon
    angle = index.astype(jnp.float32) * (2.0 * math.pi / nlon)
    scale = 1.0 / math.sqrt(nlon)
    return ((jnp.cos(angle) * scale).astype(jnp.bfloat16), (-jnp.sin(angle) * scale).astype(jnp.bfloat16))

def inverse_tables(order, nlon):
    steps = jnp.arange(nlon, dtype=jnp.int32)
    index = order[:, None] * steps[None, :] % nlon
    angle = index.astype(jnp.float32) * (2.0 * math.pi / nlon)
    factor = jnp.where(order == 0, 1.0, 2.0).astype(jnp.float32)[:, None] / math.sqrt(nlon)
    return ((jnp.cos(angle) * factor).astype(jnp.bfloat16), (-jnp.sin(angle) * factor).astype(jnp.bfloat16))

def point_layer(rows, ln_gain, mlp_in, mlp_bias, mlp_out):
    values = rows.astype(jnp.float32)
    center = lax.optimization_barrier(jnp.mean(values, axis=-1, keepdims=True))
    spread = lax.optimization_barrier(jnp.mean((values - center) ** 2, axis=-1, keepdims=True))
    normed = ((values - center) * lax.rsqrt(spread + 1e-05) * ln_gain).astype(jnp.bfloat16)
    inner = jnp.dot(normed, mlp_in, preferred_element_type=jnp.float32) + mlp_bias
    hidden = jax.nn.gelu(inner, approximate=True).astype(jnp.bfloat16)
    return (values + jnp.dot(hidden, mlp_out, preferred_element_type=jnp.float32)).astype(jnp.bfloat16)

def reference(grid, legendre, m_order, quad_weights, mix_real, mix_imag, spec_gain, ln_gain, mlp_in, mlp_bias, mlp_out):
    fwd_cos, fwd_sin = forward_tables(m_order, NLON)

    def cycle_forward(cycle):
        real_part = jnp.dot(fwd_cos.T, cycle, preferred_element_type=jnp.float32)
        imag_part = jnp.dot(fwd_sin.T, cycle, preferred_element_type=jnp.float32)
        return jnp.concatenate([real_part, imag_part], axis=1).astype(jnp.bfloat16)
    spectra = lax.map(cycle_forward, grid)
    weighted = (legendre * quad_weights[None, None, :]).astype(jnp.bfloat16)

    def order_forward(pair):
        return jnp.dot(pair[0], pair[1], preferred_element_type=jnp.float32).astype(jnp.bfloat16)
    coeffs = lax.map(order_forward, (weighted, jnp.transpose(spectra, (1, 0, 2))))
    coef_re = coeffs[:, :, :C].reshape(MODES * MODES, C)
    coef_im = coeffs[:, :, C:].reshape(MODES * MODES, C)
    mixed_re = jnp.dot(coef_re, mix_real, preferred_element_type=jnp.float32) - jnp.dot(coef_im, mix_imag, preferred_element_type=jnp.float32)
    mixed_im = jnp.dot(coef_re, mix_imag, preferred_element_type=jnp.float32) + jnp.dot(coef_im, mix_real, preferred_element_type=jnp.float32)
    filt_re = mixed_re.reshape(MODES, MODES, C) * spec_gain[None]
    filt_im = mixed_im.reshape(MODES, MODES, C) * spec_gain[None]
    filtered = jnp.concatenate([filt_re, filt_im], axis=2).astype(jnp.bfloat16)

    def order_inverse(pair):
        return jnp.dot(pair[0].T, pair[1], preferred_element_type=jnp.float32).astype(jnp.bfloat16)
    back = lax.map(order_inverse, (legendre, filtered))
    inv_cos, inv_sin = inverse_tables(m_order, NLON)

    def cycle_inverse(pair):
        cycle_spec, cycle = pair
        wave = jnp.dot(inv_cos.T, cycle_spec[:, :C], preferred_element_type=jnp.float32)
        wave = wave + jnp.dot(inv_sin.T, cycle_spec[:, C:], preferred_element_type=jnp.float32)
        return (cycle.astype(jnp.float32) + wave).astype(jnp.bfloat16)
    summed = lax.map(cycle_inverse, (jnp.transpose(back, (1, 0, 2)), grid))

    def cycle_layer(cycle):
        return point_layer(cycle, ln_gain, mlp_in, mlp_bias, mlp_out)
    return lax.map(cycle_layer, summed)
```

```python
import math

import jax
import jax.numpy as jnp
import numpy as np
import ml_dtypes
from jax import lax
from jax.experimental import pallas as pl
from jax.experimental.pallas import tpu as pltpu
from jax.sharding import PartitionSpec as P

NLON = 1440
MODES = 384
NL = 64
NX = 4
CYC = 8
ROWS = 6
CB = 128
LB = MODES // NX
LON = NLON // NX
KP = ROWS // 2
MESH = pl.DeviceIdType.MESH
BF = jnp.bfloat16
F32 = jnp.float32


def twiddles():
    index = np.arange(MODES)[:, None] * np.arange(NLON)[None, :] % NLON
    angle = index * (2.0 * math.pi / NLON)
    table = np.stack([np.cos(angle), -np.sin(angle)]) / math.sqrt(NLON)
    return table.astype(np.float32).astype(ml_dtypes.bfloat16)


def dot(a, b):
    return jnp.dot(a, b, preferred_element_type=F32)


def kernel(
    mcol,
    mrow,
    quad,
    lng,
    bias,
    grid_h,
    tw_h,
    twt_h,
    leg_h,
    mr_h,
    mi_h,
    gain_h,
    win_h,
    wout_h,
    out_h,
    grid_v,
    tw_v,
    twt_v,
    leg_v,
    legt,
    mr_v,
    mi_v,
    gain_v,
    win_v,
    wout_v,
    stage,
    sbuf,
    rbuf,
    cs,
    cr,
    wm,
    fs,
    fr,
    es,
    er,
    itab,
    xst,
    gs,
    gr,
    ov,
    load_sem,
    s_snd,
    s_rcv,
    c_snd,
    c_rcv,
    f_snd,
    f_rcv,
    e_snd,
    e_rcv,
    g_snd,
    g_rcv,
    o_sem,
):
    me = lax.axis_index("lat")
    x = lax.axis_index("ch")

    loads = [
        pltpu.make_async_copy(src, dst, load_sem.at[i])
        for i, (src, dst) in enumerate(
            [
                (tw_h, tw_v),
                (grid_h, grid_v),
                (leg_h, leg_v),
                (mr_h, mr_v),
                (mi_h, mi_v),
                (twt_h, twt_v),
                (gain_h.at[pl.ds(pl.multiple_of(x * LB, LB), LB)], gain_v),
                (win_h, win_v),
                (wout_h, wout_v),
            ]
        )
    ]
    for load in loads:
        load.start()

    barrier = pltpu.get_barrier_semaphore()

    @pl.loop(1, NL)
    def _(s):
        pl.semaphore_signal(
            barrier, inc=1, device_id=(lax.rem(me + s, NL), x), device_id_type=MESH
        )

    for s in range(1, NX):
        pl.semaphore_signal(
            barrier, inc=1, device_id=(me, lax.rem(x + s, NX)), device_id_type=MESH
        )

    def lat_send(src, dst, snd, rcv):
        @pl.loop(1, NL)
        def _(s):
            j = lax.rem(me + s, NL)
            pltpu.make_async_remote_copy(
                src_ref=src.at[j],
                dst_ref=dst.at[me],
                send_sem=snd,
                recv_sem=rcv,
                device_id=(j, x),
                device_id_type=MESH,
            ).start()

        pltpu.make_async_copy(src.at[me], dst.at[me], rcv).start()

    def ch_send(src, dst, snd, rcv):
        for s in (2, 1, 3):
            i = lax.rem(x + s, NX)
            pltpu.make_async_remote_copy(
                src_ref=src.at[i],
                dst_ref=dst.at[x],
                send_sem=snd,
                recv_sem=rcv,
                device_id=(me, i),
                device_id_type=MESH,
            ).start()
        pltpu.make_async_copy(src.at[x], dst.at[x], rcv).start()

    def take(ref, sem):
        pltpu.make_async_copy(ref, ref, sem).wait()

    loads[0].wait()
    loads[1].wait()
    lane = lax.broadcasted_iota(jnp.int32, (2 * NL, MODES), 1)
    for kp in range(KP):
        hot = jnp.where(mcol[kp * 2 * NL : (kp + 1) * 2 * NL, :] == lane, 1.0, 0.0).astype(BF)
        table = jnp.concatenate(
            [dot(hot, tw_v[0]).astype(BF), dot(hot, tw_v[1]).astype(BF)], axis=0
        )
        for p in range(CYC // 2):
            res = dot(table, jnp.concatenate([grid_v[2 * p], grid_v[2 * p + 1]], axis=1))
            for reim in range(2):
                for k2 in range(2):
                    at = (reim * 2 + k2) * NL
                    for c in range(2):
                        row = k2 * 16 + reim * 8 + 2 * p + c
                        stage[pl.ds(row, NL, stride=32), :] = res[
                            at : at + NL, c * CB : (c + 1) * CB
                        ]
        sbuf[kp] = stage[...].astype(BF).reshape(NL, 32, CB)
        if kp == 0:
            pl.semaphore_wait(barrier, NL - 1 + NX - 1)
        lat_send(sbuf.at[kp], rbuf.at[kp], s_snd.at[kp], s_rcv.at[kp])

    loads[2].wait()
    for k in range(ROWS):
        values = leg_v[k]
        legt[k] = values.T
        leg_v[k] = (values.astype(F32) * quad[...]).astype(BF)
    loads[3].wait()
    loads[4].wait()
    for xs in range(NX):
        for xd in range(NX):
            re = mr_v[xs * CB : (xs + 1) * CB, xd * CB : (xd + 1) * CB]
            im = mi_v[xs * CB : (xs + 1) * CB, xd * CB : (xd + 1) * CB]
            r0, c0 = xs * 2 * CB, xd * 2 * CB
            wm[r0 : r0 + CB, c0 : c0 + CB] = re
            wm[r0 : r0 + CB, c0 + CB : c0 + 2 * CB] = im
            wm[r0 + CB : r0 + 2 * CB, c0 : c0 + CB] = -im
            wm[r0 + CB : r0 + 2 * CB, c0 + CB : c0 + 2 * CB] = re
    loads[5].wait()
    order = lax.broadcasted_iota(jnp.int32, (MODES, MODES), 0)
    scale = jnp.where(order == 0, 1.0, 2.0)
    hot = jnp.where(mrow[...] == order, scale, 0.0).astype(BF)
    for reim in range(2):
        itab[:, reim * MODES : (reim + 1) * MODES] = dot(twt_v[reim], hot).astype(BF)
    loads[6].wait()

    upper = lax.broadcasted_iota(jnp.int32, (NL, 8, CB), 1) < 4

    def analyse(kp):
        take(rbuf.at[kp], s_rcv.at[kp])
        for k2 in range(2):
            got = rbuf[kp, :, k2 * 16 : (k2 + 1) * 16, :].astype(F32)
            spec = jnp.concatenate(
                [
                    got[:, :8, :].reshape(NL * 8, CB).astype(BF),
                    got[:, 8:, :].reshape(NL * 8, CB).astype(BF),
                ],
                axis=1,
            )
            coef = dot(leg_v[2 * kp + k2], spec).astype(BF)
            for i in range(NX):
                cs[kp, i, k2] = coef[i * LB : (i + 1) * LB]
        ch_send(cs.at[kp], cr.at[kp], c_snd.at[kp], c_rcv.at[kp])

    def mix(kp):
        take(cr.at[kp], c_rcv.at[kp])
        lhs = jnp.concatenate([cr[kp, i].reshape(2 * LB, 2 * CB) for i in range(NX)], axis=1)
        res = dot(lhs, wm[...])
        for i in range(NX):
            part = gain_v[:, i * CB : (i + 1) * CB]
            part = jnp.concatenate([part, part], axis=1)
            part = jnp.concatenate([part, part], axis=0)
            filt = (res[:, i * 2 * CB : (i + 1) * 2 * CB] * part).astype(BF)
            fs[kp, i] = filt.reshape(2, LB, 2 * CB)
        ch_send(fs.at[kp], fr.at[kp], f_snd.at[kp], f_rcv.at[kp])

    def synthesise(kp):
        take(fr.at[kp], f_rcv.at[kp])
        halves = [[], []]
        for k2 in range(2):
            filt = jnp.concatenate([fr[kp, i, k2] for i in range(NX)], axis=0)
            back = dot(legt[2 * kp + k2], filt)
            re = back[:, :CB].reshape(NL, 8, CB)
            im = back[:, CB:].reshape(NL, 8, CB)
            halves[0].append(jnp.where(upper, re, pltpu.roll(im, 4, 1)))
            halves[1].append(jnp.where(upper, pltpu.roll(re, 4, 1), im))
        for h in range(2):
            es[h, kp] = jnp.concatenate(halves[h], axis=1).astype(BF)

    def back_send(h, kp):
        lat_send(es.at[h, kp], er.at[h, kp], e_snd.at[h, kp], e_rcv.at[h, kp])

    def waves(h):
        for kp in range(KP):
            take(er.at[h, kp], e_rcv.at[h, kp])
        xst[...] = er[h].astype(F32).reshape(KP * NL * 16, CB)
        for q in range(2):
            p = 2 * h + q
            cols = []
            for c in range(2):
                cols.append(
                    jnp.concatenate(
                        [
                            xst[
                                pl.ds(kp * NL * 16 + k2 * 8 + reim * 4 + 2 * q + c, NL, stride=16),
                                :,
                            ]
                            for reim in range(2)
                            for kp in range(KP)
                            for k2 in range(2)
                        ],
                        axis=0,
                    ).astype(BF)
                )
            wave = dot(itab[...], jnp.concatenate(cols, axis=1))
            both = [grid_v[2 * p + c].astype(F32) + wave[:, c * CB : (c + 1) * CB] for c in range(2)]
            for i in range(NX):
                gs[p, i] = jnp.concatenate(
                    [b[i * LON : (i + 1) * LON] for b in both], axis=0
                ).astype(BF)
            ch_send(gs.at[p], gr.at[p], g_snd.at[p], g_rcv.at[p])

    step = 240

    def points(p):
        take(gr.at[p], g_rcv.at[p])

        @pl.loop(0, 2 * LON // step)
        def _(t):
            at = pl.ds(pl.multiple_of(t * step, 16), step)
            values = jnp.concatenate([gr[p, i, at, :] for i in range(NX)], axis=1).astype(F32)
            center = jnp.mean(values, axis=-1, keepdims=True)
            moved = values - center
            spread = jnp.mean(moved * moved, axis=-1, keepdims=True)
            normed = (moved * lax.rsqrt(spread + 1e-05) * lng[...]).astype(BF)
            inner = dot(normed, win_v[...]) + bias[...]
            hidden = jax.nn.gelu(inner, approximate=True).astype(BF)
            ov[p, at, :] = (values + dot(hidden, wout_v[...])).astype(BF)

        pltpu.make_async_copy(ov.at[p], out_h.at[p], o_sem.at[p]).start()

    for kp in range(KP):
        analyse(kp)
        mix(kp)
        synthesise(kp)
        back_send(0, kp)
    for kp in range(KP):
        back_send(1, kp)
    waves(0)
    loads[7].wait()
    loads[8].wait()
    points(0)
    points(1)
    waves(1)
    points(2)
    points(3)

    for kp in range(KP):
        take(sbuf.at[kp, pl.ds(0, NL - 1)], s_snd.at[kp])
        take(cs.at[kp, pl.ds(0, NX - 1)], c_snd.at[kp])
        take(fs.at[kp, pl.ds(0, NX - 1)], f_snd.at[kp])
        for h in range(2):
            take(es.at[h, kp, pl.ds(0, NL - 1)], e_snd.at[h, kp])
    for p in range(CYC // 2):
        take(gs.at[p, pl.ds(0, NX - 1)], g_snd.at[p])
        pltpu.make_async_copy(ov.at[p], out_h.at[p], o_sem.at[p]).wait()


def body(
    grid,
    legendre,
    m_order,
    quad_weights,
    mix_real,
    mix_imag,
    spec_gain,
    ln_gain,
    mlp_in,
    mlp_bias,
    mlp_out,
):
    table = twiddles()
    order = m_order.reshape(NL, ROWS).T.reshape(MODES)
    vm = pl.BlockSpec(memory_space=pltpu.VMEM)
    hbm = pl.BlockSpec(memory_space=pl.ANY)
    dma = pltpu.SemaphoreType.DMA
    out = pl.pallas_call(
        kernel,
        out_shape=jax.ShapeDtypeStruct((CYC // 2, 2 * LON, NX * CB), BF),
        in_specs=[vm] * 5 + [hbm] * 9,
        out_specs=hbm,
        scratch_shapes=[
            pltpu.VMEM((CYC, NLON, CB), BF),
            pltpu.VMEM((2, MODES, NLON), BF),
            pltpu.VMEM((2, NLON, MODES), BF),
            pltpu.VMEM((ROWS, MODES, NL * CYC), BF),
            pltpu.VMEM((ROWS, NL * CYC, MODES), BF),
            pltpu.VMEM(mix_real.shape, BF),
            pltpu.VMEM(mix_imag.shape, BF),
            pltpu.VMEM((LB, NX * CB), F32),
            pltpu.VMEM(mlp_in.shape, BF),
            pltpu.VMEM(mlp_out.shape, BF),
            pltpu.VMEM((NL * 32, CB), F32),
            pltpu.VMEM((KP, NL, 32, CB), BF),
            pltpu.VMEM((KP, NL, 32, CB), BF),
            pltpu.VMEM((KP, NX, 2, LB, 2 * CB), BF),
            pltpu.VMEM((KP, NX, 2, LB, 2 * CB), BF),
            pltpu.VMEM((2 * NX * CB, 2 * NX * CB), BF),
            pltpu.VMEM((KP, NX, 2, LB, 2 * CB), BF),
            pltpu.VMEM((KP, NX, 2, LB, 2 * CB), BF),
            pltpu.VMEM((2, KP, NL, 16, CB), BF),
            pltpu.VMEM((2, KP, NL, 16, CB), BF),
            pltpu.VMEM((NLON, 2 * MODES), BF),
            pltpu.VMEM((KP * NL * 16, CB), F32),
            pltpu.VMEM((CYC // 2, NX, 2 * LON, CB), BF),
            pltpu.VMEM((CYC // 2, NX, 2 * LON, CB), BF),
            pltpu.VMEM((CYC // 2, 2 * LON, NX * CB), BF),
            dma((9,)),
            dma((KP,)),
            dma((KP,)),
            dma((KP,)),
            dma((KP,)),
            dma((KP,)),
            dma((KP,)),
            dma((2, KP)),
            dma((2, KP)),
            dma((CYC // 2,)),
            dma((CYC // 2,)),
            dma((CYC // 2,)),
        ],
        compiler_params=pltpu.CompilerParams(
            collective_id=0, has_side_effects=True, vmem_limit_bytes=60 << 20
        ),
        name="sfno_block",
    )(
        order[:, None],
        order[None, :],
        quad_weights[None, :],
        ln_gain[None, :],
        mlp_bias[None, :],
        grid,
        jnp.asarray(table),
        jnp.asarray(np.ascontiguousarray(table.transpose(0, 2, 1))),
        legendre,
        mix_real,
        mix_imag,
        spec_gain,
        mlp_in,
        mlp_out,
    )
    return out.reshape(CYC, LON, NX * CB)


def solution(mesh):
    placed = (P("lat", None, "ch"), P("lat", None, None)) + (P(),) * 9
    return jax.shard_map(
        body, mesh=mesh, in_specs=placed, out_specs=P("lat", "ch", None), check_vma=False
    )
```

```python
import math

import jax
import jax.numpy as jnp
import numpy as np
import ml_dtypes
from jax import lax
from jax.experimental import pallas as pl
from jax.experimental.pallas import tpu as pltpu
from jax.sharding import PartitionSpec as P

NLON = 1440
MODES = 384
NL = 64
NX = 4
CYC = 8
ROWS = 6
CB = 128
LB = MODES // NX
LON = NLON // NX
KP = ROWS // 2
PIECES = [(0, 0, 720), (1, 0, 720), (2, 0, 720), (3, 0, 368), (3, 368, 352)]
MESH = pl.DeviceIdType.MESH
BF = jnp.bfloat16
F32 = jnp.float32


def twiddles():
    index = np.arange(MODES)[:, None] * np.arange(NLON)[None, :] % NLON
    angle = index * (2.0 * math.pi / NLON)
    table = np.stack([np.cos(angle), -np.sin(angle)]) / math.sqrt(NLON)
    return table.astype(np.float32).astype(ml_dtypes.bfloat16)


def dot(a, b):
    return jnp.dot(a, b, preferred_element_type=F32)


def kernel(
    morder,
    quad,
    lng,
    bias,
    grid_h,
    tw_h,
    twt_h,
    leg_h,
    mr_h,
    mi_h,
    gain_h,
    win_h,
    wout_h,
    out_h,
    grid_v,
    tw_v,
    twt_v,
    leg_v,
    legt,
    mr_v,
    mi_v,
    gain_v,
    win_v,
    wout_v,
    stage,
    sbuf,
    rbuf,
    cs,
    cr,
    wm,
    fs,
    fr,
    es,
    er,
    itab,
    xst,
    gs,
    gr,
    ov,
    load_sem,
    s_snd,
    s_rcv,
    c_snd,
    c_rcv,
    f_snd,
    f_rcv,
    e_snd,
    e_rcv,
    g_snd,
    g_rcv,
    o_sem,
):
    me = lax.axis_index("lat")
    x = lax.axis_index("ch")

    loads = [
        pltpu.make_async_copy(src, dst, load_sem.at[i])
        for i, (src, dst) in enumerate(
            [
                (tw_h, tw_v),
                (grid_h, grid_v),
                (leg_h, leg_v),
                (mr_h, mr_v),
                (mi_h, mi_v),
                (twt_h, twt_v),
                (gain_h.at[pl.ds(pl.multiple_of(x * LB, LB), LB)], gain_v),
                (win_h, win_v),
                (wout_h, wout_v),
            ]
        )
    ]
    for load in loads:
        load.start()

    barrier = pltpu.get_barrier_semaphore()

    @pl.loop(1, NL)
    def _(s):
        pl.semaphore_signal(
            barrier, inc=1, device_id=(lax.rem(me + s, NL), x), device_id_type=MESH
        )

    for s in range(1, NX):
        pl.semaphore_signal(
            barrier, inc=1, device_id=(me, lax.rem(x + s, NX)), device_id_type=MESH
        )

    def lat_send(src, dst, snd, rcv):
        @pl.loop(1, NL)
        def _(s):
            j = lax.rem(me + s, NL)
            pltpu.make_async_remote_copy(
                src_ref=src.at[j],
                dst_ref=dst.at[me],
                send_sem=snd,
                recv_sem=rcv,
                device_id=(j, x),
                device_id_type=MESH,
            ).start()

        pltpu.make_async_copy(src.at[me], dst.at[me], rcv).start()

    def ch_send(src, dst, snd, rcv):
        for s in (2, 1, 3):
            i = lax.rem(x + s, NX)
            pltpu.make_async_remote_copy(
                src_ref=src.at[i],
                dst_ref=dst.at[x],
                send_sem=snd,
                recv_sem=rcv,
                device_id=(me, i),
                device_id_type=MESH,
            ).start()
        pltpu.make_async_copy(src.at[x], dst.at[x], rcv).start()

    def take(ref, sem):
        pltpu.make_async_copy(ref, ref, sem).wait()

    order = lax.broadcasted_iota(jnp.int32, (MODES, MODES), 0)
    place = lax.broadcasted_iota(jnp.int32, (MODES, MODES), 1)
    moved = jnp.where(order == ROWS * (place % NL) + place // NL, 1.0, 0.0).astype(BF)
    hot = dot(jnp.where(morder[...] == order, 1.0, 0.0).astype(BF), moved)
    pick = hot.T.astype(BF)

    loads[0].wait()
    loads[1].wait()
    for kp in range(KP):
        rows = pick[kp * 2 * NL : (kp + 1) * 2 * NL]
        table = jnp.concatenate(
            [dot(rows, tw_v[0]).astype(BF), dot(rows, tw_v[1]).astype(BF)], axis=0
        )
        for p in range(CYC // 2):
            res = dot(table, jnp.concatenate([grid_v[2 * p], grid_v[2 * p + 1]], axis=1))
            for reim in range(2):
                for k2 in range(2):
                    at = (reim * 2 + k2) * NL
                    for c in range(2):
                        row = k2 * NL * 16 + reim * 8 + 2 * p + c
                        stage[pl.ds(row, NL, stride=16), :] = res[
                            at : at + NL, c * CB : (c + 1) * CB
                        ]
        for k2 in range(2):
            part = stage[k2 * NL * 16 : (k2 + 1) * NL * 16]
            sbuf[2 * kp + k2] = part.astype(BF).reshape(NL, 16, CB)
        if kp == 0:
            pl.semaphore_wait(barrier, NL - 1 + NX - 1)
        for k in (2 * kp, 2 * kp + 1):
            lat_send(sbuf.at[k], rbuf.at[k], s_snd.at[k], s_rcv.at[k])

    loads[2].wait()
    for k in range(ROWS):
        values = leg_v[k]
        legt[k] = values.T
        leg_v[k] = (values.astype(F32) * quad[...]).astype(BF)
    loads[3].wait()
    loads[4].wait()
    for xs in range(NX):
        for xd in range(NX):
            re = mr_v[xs * CB : (xs + 1) * CB, xd * CB : (xd + 1) * CB]
            im = mi_v[xs * CB : (xs + 1) * CB, xd * CB : (xd + 1) * CB]
            r0, c0 = xs * 2 * CB, xd * 2 * CB
            wm[r0 : r0 + CB, c0 : c0 + CB] = re
            wm[r0 : r0 + CB, c0 + CB : c0 + 2 * CB] = im
            wm[r0 + CB : r0 + 2 * CB, c0 : c0 + CB] = -im
            wm[r0 + CB : r0 + 2 * CB, c0 + CB : c0 + 2 * CB] = re
    loads[5].wait()
    hot = (hot * jnp.where(order == 0, 1.0, 2.0)).astype(BF)
    for reim in range(2):
        itab[:, reim * MODES : (reim + 1) * MODES] = dot(twt_v[reim], hot).astype(BF)
    loads[6].wait()

    upper = lax.broadcasted_iota(jnp.int32, (NL, 8, CB), 1) < 4

    def analyse(k):
        got = rbuf[k].astype(F32)
        spec = jnp.concatenate(
            [
                got[:, :8, :].reshape(NL * 8, CB).astype(BF),
                got[:, 8:, :].reshape(NL * 8, CB).astype(BF),
            ],
            axis=1,
        )
        cs[k] = dot(leg_v[k], spec).astype(BF).reshape(NX, LB, 2 * CB)
        ch_send(cs.at[k], cr.at[k], c_snd.at[k], c_rcv.at[k])

    def mix(k):
        take(cr.at[k], c_rcv.at[k])
        res = dot(jnp.concatenate([cr[k, i] for i in range(NX)], axis=1), wm[...])
        for i in range(NX):
            part = gain_v[:, i * CB : (i + 1) * CB]
            part = jnp.concatenate([part, part], axis=1)
            fs[k, i] = (res[:, i * 2 * CB : (i + 1) * 2 * CB] * part).astype(BF)
        ch_send(fs.at[k], fr.at[k], f_snd.at[k], f_rcv.at[k])

    def synthesise(k):
        take(fr.at[k], f_rcv.at[k])
        back = dot(legt[k], fr[k].reshape(MODES, 2 * CB))
        re = back[:, :CB].reshape(NL, 8, CB)
        im = back[:, CB:].reshape(NL, 8, CB)
        return (
            jnp.where(upper, re, pltpu.roll(im, 4, 1)),
            jnp.where(upper, pltpu.roll(re, 4, 1), im),
        )

    def pack(kp, first, second):
        for h in range(2):
            es[h, kp] = jnp.concatenate([first[h], second[h]], axis=1).astype(BF)

    def back_send(h, kp):
        lat_send(es.at[h, kp], er.at[h, kp], e_snd.at[h, kp], e_rcv.at[h, kp])

    def waves(h):
        for kp in range(KP):
            take(er.at[h, kp], e_rcv.at[h, kp])
        xst[...] = er[h].astype(F32).reshape(KP * NL * 16, CB)
        for q in range(2):
            p = 2 * h + q
            cols = []
            for c in range(2):
                cols.append(
                    jnp.concatenate(
                        [
                            xst[
                                pl.ds(kp * NL * 16 + k2 * 8 + reim * 4 + 2 * q + c, NL, stride=16),
                                :,
                            ]
                            for reim in range(2)
                            for kp in range(KP)
                            for k2 in range(2)
                        ],
                        axis=0,
                    ).astype(BF)
                )
            wave = dot(itab[...], jnp.concatenate(cols, axis=1))
            both = [grid_v[2 * p + c].astype(F32) + wave[:, c * CB : (c + 1) * CB] for c in range(2)]
            for i in range(NX):
                gs[p, i] = jnp.concatenate(
                    [b[i * LON : (i + 1) * LON] for b in both], axis=0
                ).astype(BF)
            for t, (pair, at, n) in enumerate(PIECES):
                if pair == p:
                    part = pl.ds(at, n)
                    ch_send(
                        gs.at[p, :, part], gr.at[p, :, part], g_snd.at[t], g_rcv.at[t]
                    )

    def points(t):
        p, at, n = PIECES[t]
        part = pl.ds(at, n)
        take(gr.at[p, :, part], g_rcv.at[t])
        values = jnp.concatenate([gr[p, i, part, :] for i in range(NX)], axis=1).astype(F32)
        center = jnp.mean(values, axis=-1, keepdims=True)
        moved = values - center
        spread = jnp.mean(moved * moved, axis=-1, keepdims=True)
        normed = (moved * lax.rsqrt(spread + 1e-05) * lng[...]).astype(BF)
        inner = dot(normed, win_v[...]) + bias[...]
        hidden = jax.nn.gelu(inner, approximate=True).astype(BF)
        ov[p, part, :] = (values + dot(hidden, wout_v[...])).astype(BF)
        pltpu.make_async_copy(ov.at[p, part], out_h.at[p, part], o_sem.at[t]).start()

    for kp in range(KP):
        a, b = 2 * kp, 2 * kp + 1
        take(rbuf.at[a], s_rcv.at[a])
        analyse(a)
        mix(a)
        take(rbuf.at[b], s_rcv.at[b])
        analyse(b)
        if kp == KP - 1:
            back_send(0, 0)
            back_send(0, 1)
        first = synthesise(a)
        mix(b)
        pack(kp, first, synthesise(b))
    back_send(0, KP - 1)
    for kp in range(KP):
        back_send(1, kp)
    loads[7].wait()
    loads[8].wait()
    waves(0)
    points(0)
    waves(1)
    for t in range(1, len(PIECES)):
        points(t)

    for k in range(ROWS):
        take(sbuf.at[k, pl.ds(0, NL - 1)], s_snd.at[k])
        take(cs.at[k, pl.ds(0, NX - 1)], c_snd.at[k])
        take(fs.at[k, pl.ds(0, NX - 1)], f_snd.at[k])
    for kp in range(KP):
        for h in range(2):
            take(es.at[h, kp, pl.ds(0, NL - 1)], e_snd.at[h, kp])
    for t, (p, at, n) in enumerate(PIECES):
        part = pl.ds(at, n)
        take(gs.at[p, pl.ds(0, NX - 1), part], g_snd.at[t])
        pltpu.make_async_copy(ov.at[p, part], out_h.at[p, part], o_sem.at[t]).wait()


def body(
    grid,
    legendre,
    m_order,
    quad_weights,
    mix_real,
    mix_imag,
    spec_gain,
    ln_gain,
    mlp_in,
    mlp_bias,
    mlp_out,
):
    table = twiddles()
    vm = pl.BlockSpec(memory_space=pltpu.VMEM)
    hbm = pl.BlockSpec(memory_space=pl.ANY)
    dma = pltpu.SemaphoreType.DMA
    out = pl.pallas_call(
        kernel,
        out_shape=jax.ShapeDtypeStruct((CYC // 2, 2 * LON, NX * CB), BF),
        in_specs=[vm] * 4 + [hbm] * 9,
        out_specs=hbm,
        scratch_shapes=[
            pltpu.VMEM((CYC, NLON, CB), BF),
            pltpu.VMEM((2, MODES, NLON), BF),
            pltpu.VMEM((2, NLON, MODES), BF),
            pltpu.VMEM((ROWS, MODES, NL * CYC), BF),
            pltpu.VMEM((ROWS, NL * CYC, MODES), BF),
            pltpu.VMEM(mix_real.shape, BF),
            pltpu.VMEM(mix_imag.shape, BF),
            pltpu.VMEM((LB, NX * CB), F32),
            pltpu.VMEM(mlp_in.shape, BF),
            pltpu.VMEM(mlp_out.shape, BF),
            pltpu.VMEM((NL * 32, CB), F32),
            pltpu.VMEM((ROWS, NL, 16, CB), BF),
            pltpu.VMEM((ROWS, NL, 16, CB), BF),
            pltpu.VMEM((ROWS, NX, LB, 2 * CB), BF),
            pltpu.VMEM((ROWS, NX, LB, 2 * CB), BF),
            pltpu.VMEM((2 * NX * CB, 2 * NX * CB), BF),
            pltpu.VMEM((ROWS, NX, LB, 2 * CB), BF),
            pltpu.VMEM((ROWS, NX, LB, 2 * CB), BF),
            pltpu.VMEM((2, KP, NL, 16, CB), BF),
            pltpu.VMEM((2, KP, NL, 16, CB), BF),
            pltpu.VMEM((NLON, 2 * MODES), BF),
            pltpu.VMEM((KP * NL * 16, CB), F32),
            pltpu.VMEM((CYC // 2, NX, 2 * LON, CB), BF),
            pltpu.VMEM((CYC // 2, NX, 2 * LON, CB), BF),
            pltpu.VMEM((CYC // 2, 2 * LON, NX * CB), BF),
            dma((9,)),
            dma((ROWS,)),
            dma((ROWS,)),
            dma((ROWS,)),
            dma((ROWS,)),
            dma((ROWS,)),
            dma((ROWS,)),
            dma((2, KP)),
            dma((2, KP)),
            dma((len(PIECES),)),
            dma((len(PIECES),)),
            dma((len(PIECES),)),
        ],
        compiler_params=pltpu.CompilerParams(
            collective_id=0, has_side_effects=True, vmem_limit_bytes=60 << 20
        ),
        name="sfno_block",
    )(
        m_order[None, :],
        quad_weights[None, :],
        ln_gain[None, :],
        mlp_bias[None, :],
        grid,
        jnp.asarray(table),
        jnp.asarray(np.ascontiguousarray(table.transpose(0, 2, 1))),
        legendre,
        mix_real,
        mix_imag,
        spec_gain,
        mlp_in,
        mlp_out,
    )
    return out.reshape(CYC, LON, NX * CB)


def solution(mesh):
    placed = (P("lat", None, "ch"), P("lat", None, None)) + (P(),) * 9
    return jax.shard_map(
        body, mesh=mesh, in_specs=placed, out_specs=P("lat", "ch", None), check_vma=False
    )
```

```python
import math

import jax
import jax.numpy as jnp
import numpy as np
import ml_dtypes
from jax import lax
from jax.experimental import pallas as pl
from jax.experimental.pallas import tpu as pltpu
from jax.sharding import PartitionSpec as P

NLON = 1440
MODES = 384
NL = 64
NX = 4
CYC = 8
ROWS = 6
CB = 128
LB = MODES // NX
LON = NLON // NX
KP = ROWS // 2
PIECES = [(0, 0, 720), (1, 0, 720), (2, 0, 720), (3, 0, 368), (3, 368, 352)]
MESH = pl.DeviceIdType.MESH
BF = jnp.bfloat16
F32 = jnp.float32


def twiddles():
    index = np.arange(MODES)[:, None] * np.arange(NLON)[None, :] % NLON
    angle = index * (2.0 * math.pi / NLON)
    table = np.stack([np.cos(angle), -np.sin(angle)]) / math.sqrt(NLON)
    return table.astype(np.float32).astype(ml_dtypes.bfloat16)


def dot(a, b):
    return jnp.dot(a, b, preferred_element_type=F32)


def point_layer(rows, lng, win, bias, wout):
    values = rows.astype(F32)
    center = jnp.mean(values, axis=-1, keepdims=True)
    moved = values - center
    spread = jnp.mean(moved * moved, axis=-1, keepdims=True)
    normed = (moved * lax.rsqrt(spread + 1e-05) * lng[...]).astype(BF)
    inner = dot(normed, win[...]) + bias[...]
    hidden = jax.nn.gelu(inner, approximate=True).astype(BF)
    return (values + dot(hidden, wout[...])).astype(BF)


def finish(lng, bias, win_h, wout_h, last_h, part_h, out_h, win, wout, last, hold, l_sem, i_sem, o_sem):
    p, at, n = PIECES[-1]
    loads = [
        pltpu.make_async_copy(src, dst, l_sem.at[i])
        for i, (src, dst) in enumerate([(last_h, last), (win_h, win), (wout_h, wout)])
    ]
    for load in loads:
        load.start()

    def move(t, src, dst, sem):
        pair, first, rows = PIECES[t]
        part = pl.ds(first, rows)
        return pltpu.make_async_copy(src.at[pair, part], dst.at[pair, part], sem.at[t])

    others = range(len(PIECES) - 1)
    for t in others:
        move(t, part_h, hold, i_sem).start()
    for t in others:
        move(t, part_h, hold, i_sem).wait()
        move(t, hold, out_h, o_sem).start()
    for load in loads:
        load.wait()
    rows = jnp.concatenate([last[i] for i in range(NX)], axis=1)
    hold[p, at : at + n, :] = point_layer(rows, lng, win, bias, wout)
    move(len(PIECES) - 1, hold, out_h, o_sem).start()
    for t in range(len(PIECES)):
        move(t, hold, out_h, o_sem).wait()


def kernel(
    morder,
    quad,
    lng,
    bias,
    grid_h,
    tw_h,
    twt_h,
    leg_h,
    mr_h,
    mi_h,
    gain_h,
    win_h,
    wout_h,
    out_h,
    last_h,
    grid_v,
    tw_v,
    twt_v,
    leg_v,
    legt,
    mr_v,
    mi_v,
    gain_v,
    win_v,
    wout_v,
    stage,
    sbuf,
    rbuf,
    cs,
    cr,
    wm,
    fs,
    fr,
    eq,
    rq,
    eh,
    rh,
    itab,
    xst,
    gs,
    gr,
    ov,
    load_sem,
    s_snd,
    s_rcv,
    c_snd,
    c_rcv,
    f_snd,
    f_rcv,
    q_snd,
    q_rcv,
    h_snd,
    h_rcv,
    g_snd,
    g_rcv,
    o_sem,
):
    me = lax.axis_index("lat")
    x = lax.axis_index("ch")

    loads = [
        pltpu.make_async_copy(src, dst, load_sem.at[i])
        for i, (src, dst) in enumerate(
            [
                (tw_h, tw_v),
                (grid_h, grid_v),
                (leg_h, leg_v),
                (mr_h, mr_v),
                (mi_h, mi_v),
                (twt_h, twt_v),
                (gain_h.at[pl.ds(pl.multiple_of(x * LB, LB), LB)], gain_v),
                (win_h, win_v),
                (wout_h, wout_v),
            ]
        )
    ]
    for load in loads:
        load.start()

    barrier = pltpu.get_barrier_semaphore()

    @pl.loop(1, NL)
    def _(s):
        pl.semaphore_signal(
            barrier, inc=1, device_id=(lax.rem(me + s, NL), x), device_id_type=MESH
        )

    for s in range(1, NX):
        pl.semaphore_signal(
            barrier, inc=1, device_id=(me, lax.rem(x + s, NX)), device_id_type=MESH
        )

    def lat_send(src, dst, snd, rcv):
        @pl.loop(1, NL)
        def _(s):
            j = lax.rem(me + s, NL)
            pltpu.make_async_remote_copy(
                src_ref=src.at[j],
                dst_ref=dst.at[me],
                send_sem=snd,
                recv_sem=rcv,
                device_id=(j, x),
                device_id_type=MESH,
            ).start()

        pltpu.make_async_copy(src.at[me], dst.at[me], rcv).start()

    def ch_send(src, dst, snd, rcv):
        for s in (2, 1, 3):
            i = lax.rem(x + s, NX)
            pltpu.make_async_remote_copy(
                src_ref=src.at[i],
                dst_ref=dst.at[x],
                send_sem=snd,
                recv_sem=rcv,
                device_id=(me, i),
                device_id_type=MESH,
            ).start()
        pltpu.make_async_copy(src.at[x], dst.at[x], rcv).start()

    def take(ref, sem):
        pltpu.make_async_copy(ref, ref, sem).wait()

    order = lax.broadcasted_iota(jnp.int32, (MODES, MODES), 0)
    place = lax.broadcasted_iota(jnp.int32, (MODES, MODES), 1)
    moved = jnp.where(order == ROWS * (place % NL) + place // NL, 1.0, 0.0).astype(BF)
    hot = dot(jnp.where(morder[...].reshape(1, MODES) == order, 1.0, 0.0).astype(BF), moved)
    pick = hot.T.astype(BF)

    loads[0].wait()
    loads[1].wait()
    for kp in range(KP):
        rows = pick[kp * 2 * NL : (kp + 1) * 2 * NL]
        table = jnp.concatenate(
            [dot(rows, tw_v[0]).astype(BF), dot(rows, tw_v[1]).astype(BF)], axis=0
        )
        for p in range(CYC // 2):
            res = dot(table, jnp.concatenate([grid_v[2 * p], grid_v[2 * p + 1]], axis=1))
            for reim in range(2):
                for k2 in range(2):
                    at = (reim * 2 + k2) * NL
                    for c in range(2):
                        row = k2 * NL * 16 + reim * 8 + 2 * p + c
                        stage[pl.ds(row, NL, stride=16), :] = res[
                            at : at + NL, c * CB : (c + 1) * CB
                        ]
        for k2 in range(2):
            part = stage[k2 * NL * 16 : (k2 + 1) * NL * 16]
            sbuf[2 * kp + k2] = part.astype(BF).reshape(NL, 16, CB)
        if kp == 0:
            pl.semaphore_wait(barrier, NL - 1 + NX - 1)
        for k in (2 * kp, 2 * kp + 1):
            lat_send(sbuf.at[k], rbuf.at[k], s_snd.at[k], s_rcv.at[k])

    loads[2].wait()
    for k in range(ROWS):
        values = leg_v[k]
        legt[k] = values.T
        leg_v[k] = (values.astype(F32) * quad[...]).astype(BF)
    loads[3].wait()
    loads[4].wait()
    for xs in range(NX):
        for xd in range(NX):
            re = mr_v[xs * CB : (xs + 1) * CB, xd * CB : (xd + 1) * CB]
            im = mi_v[xs * CB : (xs + 1) * CB, xd * CB : (xd + 1) * CB]
            r0, c0 = xs * 2 * CB, xd * 2 * CB
            wm[r0 : r0 + CB, c0 : c0 + CB] = re
            wm[r0 : r0 + CB, c0 + CB : c0 + 2 * CB] = im
            wm[r0 + CB : r0 + 2 * CB, c0 : c0 + CB] = -im
            wm[r0 + CB : r0 + 2 * CB, c0 + CB : c0 + 2 * CB] = re
    loads[5].wait()
    hot = (hot * jnp.where(order == 0, 1.0, 2.0)).astype(BF)
    for reim in range(2):
        itab[:, reim * MODES : (reim + 1) * MODES] = dot(twt_v[reim], hot).astype(BF)
    loads[6].wait()

    sub = lax.broadcasted_iota(jnp.int32, (NL, 8, CB), 1)

    def analyse(k):
        got = rbuf[k].astype(F32)
        spec = jnp.concatenate(
            [
                got[:, :8, :].reshape(NL * 8, CB).astype(BF),
                got[:, 8:, :].reshape(NL * 8, CB).astype(BF),
            ],
            axis=1,
        )
        cs[k] = dot(leg_v[k], spec).astype(BF).reshape(NX, LB, 2 * CB)
        ch_send(cs.at[k], cr.at[k], c_snd.at[k], c_rcv.at[k])

    def mix(k):
        take(cr.at[k], c_rcv.at[k])
        res = dot(jnp.concatenate([cr[k, i] for i in range(NX)], axis=1), wm[...])
        for i in range(NX):
            part = gain_v[:, i * CB : (i + 1) * CB]
            part = jnp.concatenate([part, part], axis=1)
            fs[k, i] = (res[:, i * 2 * CB : (i + 1) * 2 * CB] * part).astype(BF)
        ch_send(fs.at[k], fr.at[k], f_snd.at[k], f_rcv.at[k])

    def synthesise(k):
        take(fr.at[k], f_rcv.at[k])
        back = dot(legt[k], fr[k].reshape(MODES, 2 * CB))
        return back[:, :CB].reshape(NL, 8, CB), back[:, CB:].reshape(NL, 8, CB)

    def gather(parts, first, n):
        out = None
        for i, part in enumerate(parts):
            turned = pltpu.roll(part, (n * i - first) % 8, 1)
            out = turned if out is None else jnp.where(sub < n * i, out, turned)
        return out

    def pack_quarters(backs):
        for g in range(4):
            tiles = [
                gather([*backs[2 * i], *backs[2 * i + 1]], 2 * g, 2) for i in range(2)
            ]
            eq[g] = jnp.concatenate(tiles, axis=1).astype(BF)

    def pack_halves(backs):
        for h in range(2):
            tiles = [gather(backs[i], 4 * h, 4) for i in range(2)]
            eh[h] = jnp.concatenate(tiles, axis=1).astype(BF)

    def send_quarter(g):
        lat_send(eq.at[g], rq.at[g], q_snd.at[g], q_rcv.at[g])

    def send_half(h):
        lat_send(eh.at[h], rh.at[h], h_snd.at[h], h_rcv.at[h])

    def waves(p):
        take(rq.at[p], q_rcv.at[p])
        if p % 2 == 0:
            take(rh.at[p // 2], h_rcv.at[p // 2])
        xst[: NL * 16] = rq[p].astype(F32).reshape(NL * 16, CB)
        xst[NL * 16 :] = rh[p // 2].astype(F32).reshape(NL * 16, CB)
        cols = []
        for c in range(2):
            part = []
            for reim in range(2):
                for k in range(4):
                    part.append(xst[pl.ds(k * 4 + reim * 2 + c, NL, stride=16), :])
                for k in range(2):
                    at = NL * 16 + k * 8 + reim * 4 + 2 * (p % 2) + c
                    part.append(xst[pl.ds(at, NL, stride=16), :])
            cols.append(jnp.concatenate(part, axis=0).astype(BF))
        wave = dot(itab[...], jnp.concatenate(cols, axis=1))
        both = [grid_v[2 * p + c].astype(F32) + wave[:, c * CB : (c + 1) * CB] for c in range(2)]
        for i in range(NX):
            gs[p, i] = jnp.concatenate(
                [b[i * LON : (i + 1) * LON] for b in both], axis=0
            ).astype(BF)
        for t, (pair, at, n) in enumerate(PIECES):
            if pair == p:
                part = pl.ds(at, n)
                ch_send(
                    gs.at[p, :, part], gr.at[p, :, part], g_snd.at[t], g_rcv.at[t]
                )


    def points(t):
        p, at, n = PIECES[t]
        part = pl.ds(at, n)
        take(gr.at[p, :, part], g_rcv.at[t])
        if t == len(PIECES) - 1:
            copy = pltpu.make_async_copy(gr.at[p, :, part], last_h, o_sem.at[t])
        else:
            rows = jnp.concatenate([gr[p, i, part, :] for i in range(NX)], axis=1)
            ov[p, part, :] = point_layer(rows, lng, win_v, bias, wout_v)
            copy = pltpu.make_async_copy(ov.at[p, part], out_h.at[p, part], o_sem.at[t])
        copy.start()
        return copy

    backs = []
    for kp in range(KP):
        a, b = 2 * kp, 2 * kp + 1
        take(rbuf.at[a], s_rcv.at[a])
        analyse(a)
        mix(a)
        take(rbuf.at[b], s_rcv.at[b])
        analyse(b)
        if kp == KP - 1:
            send_quarter(0)
            send_quarter(1)
        backs.append(synthesise(a))
        mix(b)
        backs.append(synthesise(b))
        if kp == 1:
            pack_quarters(backs)
    pack_halves(backs[4:])
    send_half(0)
    send_half(1)
    send_quarter(2)
    send_quarter(3)
    loads[7].wait()
    loads[8].wait()
    waves(0)
    waves(1)
    copies = [points(0)]
    waves(2)
    waves(3)
    copies += [points(t) for t in range(1, len(PIECES))]

    for k in range(ROWS):
        take(sbuf.at[k, pl.ds(0, NL - 1)], s_snd.at[k])
        take(cs.at[k, pl.ds(0, NX - 1)], c_snd.at[k])
        take(fs.at[k, pl.ds(0, NX - 1)], f_snd.at[k])
    for g in range(4):
        take(eq.at[g, pl.ds(0, NL - 1)], q_snd.at[g])
    for h in range(2):
        take(eh.at[h, pl.ds(0, NL - 1)], h_snd.at[h])
    for t, (p, at, n) in enumerate(PIECES):
        part = pl.ds(at, n)
        take(gs.at[p, pl.ds(0, NX - 1), part], g_snd.at[t])
    for copy in copies:
        copy.wait()


def body(
    grid,
    legendre,
    m_order,
    quad_weights,
    mix_real,
    mix_imag,
    spec_gain,
    ln_gain,
    mlp_in,
    mlp_bias,
    mlp_out,
):
    table = twiddles()
    vm = pl.BlockSpec(memory_space=pltpu.VMEM)
    hbm = pl.BlockSpec(memory_space=pl.ANY)
    dma = pltpu.SemaphoreType.DMA
    part, last = pl.pallas_call(
        kernel,
        out_shape=[
            jax.ShapeDtypeStruct((CYC // 2, 2 * LON, NX * CB), BF),
            jax.ShapeDtypeStruct((NX, PIECES[-1][2], CB), BF),
        ],
        in_specs=[vm] * 4 + [hbm] * 9,
        out_specs=[hbm] * 2,
        scratch_shapes=[
            pltpu.VMEM((CYC, NLON, CB), BF),
            pltpu.VMEM((2, MODES, NLON), BF),
            pltpu.VMEM((2, NLON, MODES), BF),
            pltpu.VMEM((ROWS, MODES, NL * CYC), BF),
            pltpu.VMEM((ROWS, NL * CYC, MODES), BF),
            pltpu.VMEM(mix_real.shape, BF),
            pltpu.VMEM(mix_imag.shape, BF),
            pltpu.VMEM((LB, NX * CB), F32),
            pltpu.VMEM(mlp_in.shape, BF),
            pltpu.VMEM(mlp_out.shape, BF),
            pltpu.VMEM((NL * 32, CB), F32),
            pltpu.VMEM((ROWS, NL, 16, CB), BF),
            pltpu.VMEM((ROWS, NL, 16, CB), BF),
            pltpu.VMEM((ROWS, NX, LB, 2 * CB), BF),
            pltpu.VMEM((ROWS, NX, LB, 2 * CB), BF),
            pltpu.VMEM((2 * NX * CB, 2 * NX * CB), BF),
            pltpu.VMEM((ROWS, NX, LB, 2 * CB), BF),
            pltpu.VMEM((ROWS, NX, LB, 2 * CB), BF),
            pltpu.VMEM((4, NL, 16, CB), BF),
            pltpu.VMEM((4, NL, 16, CB), BF),
            pltpu.VMEM((2, NL, 16, CB), BF),
            pltpu.VMEM((2, NL, 16, CB), BF),
            pltpu.VMEM((NLON, 2 * MODES), BF),
            pltpu.VMEM((2 * NL * 16, CB), F32),
            pltpu.VMEM((CYC // 2, NX, 2 * LON, CB), BF),
            pltpu.VMEM((CYC // 2, NX, 2 * LON, CB), BF),
            pltpu.VMEM((CYC // 2, 2 * LON, NX * CB), BF),
            dma((9,)),
            dma((ROWS,)),
            dma((ROWS,)),
            dma((ROWS,)),
            dma((ROWS,)),
            dma((ROWS,)),
            dma((ROWS,)),
            dma((4,)),
            dma((4,)),
            dma((2,)),
            dma((2,)),
            dma((len(PIECES),)),
            dma((len(PIECES),)),
            dma((len(PIECES),)),
        ],
        compiler_params=pltpu.CompilerParams(
            collective_id=0, has_side_effects=True, vmem_limit_bytes=60 << 20
        ),
        name="sfno_block",
    )(
        m_order,
        quad_weights[None, :],
        ln_gain[None, :],
        mlp_bias[None, :],
        grid,
        jnp.asarray(table),
        jnp.asarray(np.ascontiguousarray(table.transpose(0, 2, 1))),
        legendre,
        mix_real,
        mix_imag,
        spec_gain,
        mlp_in,
        mlp_out,
    )
    out = pl.pallas_call(
        finish,
        out_shape=jax.ShapeDtypeStruct(part.shape, BF),
        in_specs=[vm] * 2 + [hbm] * 4,
        out_specs=hbm,
        scratch_shapes=[
            pltpu.VMEM(mlp_in.shape, BF),
            pltpu.VMEM(mlp_out.shape, BF),
            pltpu.VMEM(last.shape, BF),
            pltpu.VMEM(part.shape, BF),
            dma((3,)),
            dma((len(PIECES),)),
            dma((len(PIECES),)),
        ],
        compiler_params=pltpu.CompilerParams(vmem_limit_bytes=60 << 20),
        name="last_points",
    )(ln_gain[None, :], mlp_bias[None, :], mlp_in, mlp_out, last, part)
    return out.reshape(CYC, LON, NX * CB)


def solution(mesh):
    placed = (P("lat", None, "ch"), P("lat", None, None)) + (P(),) * 9
    return jax.shard_map(
        body, mesh=mesh, in_specs=placed, out_specs=P("lat", "ch", None), check_vma=False
    )
```

```python
import math

import jax
import jax.numpy as jnp
import numpy as np
import ml_dtypes
from jax import lax
from jax.experimental import pallas as pl
from jax.experimental.pallas import tpu as pltpu
from jax.sharding import PartitionSpec as P

NLON = 1440
MODES = 384
NL = 64
NX = 4
CYC = 8
ROWS = 6
CB = 128
LB = MODES // NX
LON = NLON // NX
KP = ROWS // 2
PIECES = [(0, 0, 720), (1, 0, 720), (2, 0, 720), (3, 0, 256), (3, 256, 256), (3, 512, 208)]
MESH = pl.DeviceIdType.MESH
BF = jnp.bfloat16
F32 = jnp.float32


def twiddles():
    index = np.arange(MODES)[:, None] * np.arange(NLON)[None, :] % NLON
    angle = index * (2.0 * math.pi / NLON)
    table = np.stack([np.cos(angle), -np.sin(angle)]) / math.sqrt(NLON)
    return table.astype(np.float32).astype(ml_dtypes.bfloat16)


def dot(a, b):
    return jnp.dot(a, b, preferred_element_type=F32)


def point_layer(rows, lng, win, bias, wout):
    values = rows.astype(F32)
    center = jnp.mean(values, axis=-1, keepdims=True)
    moved = values - center
    spread = jnp.mean(moved * moved, axis=-1, keepdims=True)
    normed = (moved * lax.rsqrt(spread + 1e-05) * lng[...]).astype(BF)
    inner = dot(normed, win[...]) + bias[...]
    half = 0.5 * inner
    root = math.sqrt(2.0 / math.pi)
    bent = jnp.tanh(inner * (root + (root * 0.044715) * (inner * inner)))
    hidden = (half + half * bent).astype(BF)
    return (values + dot(hidden, wout[...])).astype(BF)


def finish(part_h, out_h, hold, i_sem, o_sem):
    pairs = range(CYC // 2)
    into = [pltpu.make_async_copy(part_h.at[p], hold.at[p], i_sem.at[p]) for p in pairs]
    out = [pltpu.make_async_copy(hold.at[p], out_h.at[p], o_sem.at[p]) for p in pairs]
    for copy in into:
        copy.start()
    for p in pairs:
        into[p].wait()
        out[p].start()
    for copy in out:
        copy.wait()


def kernel(
    morder,
    quad,
    lng,
    bias,
    grid_h,
    tw_h,
    twt_h,
    leg_h,
    mr_h,
    mi_h,
    gain_h,
    win_h,
    wout_h,
    out_h,
    grid_v,
    tw_v,
    twt_v,
    leg_v,
    legt,
    mr_v,
    mi_v,
    gain_v,
    win_v,
    wout_v,
    stage,
    sbuf,
    rbuf,
    cs,
    cr,
    wm,
    fs,
    fr,
    eq,
    rq,
    eh,
    rh,
    itab,
    xst,
    gs,
    gr,
    ov,
    load_sem,
    s_snd,
    s_rcv,
    c_snd,
    c_rcv,
    f_snd,
    f_rcv,
    q_snd,
    q_rcv,
    h_snd,
    h_rcv,
    g_snd,
    g_rcv,
    o_sem,
):
    me = lax.axis_index("lat")
    x = lax.axis_index("ch")

    loads = [
        pltpu.make_async_copy(src, dst, load_sem.at[i])
        for i, (src, dst) in enumerate(
            [
                (tw_h, tw_v),
                (grid_h, grid_v),
                (leg_h, leg_v),
                (mr_h, mr_v),
                (mi_h, mi_v),
                (twt_h, twt_v),
                (gain_h.at[pl.ds(pl.multiple_of(x * LB, LB), LB)], gain_v),
                (win_h, win_v),
                (wout_h, wout_v),
            ]
        )
    ]
    for load in loads:
        load.start()

    barrier = pltpu.get_barrier_semaphore()

    @pl.loop(1, NL)
    def _(s):
        pl.semaphore_signal(
            barrier, inc=1, device_id=(lax.rem(me + s, NL), x), device_id_type=MESH
        )

    for s in range(1, NX):
        pl.semaphore_signal(
            barrier, inc=1, device_id=(me, lax.rem(x + s, NX)), device_id_type=MESH
        )

    def lat_send(src, dst, snd, rcv):
        @pl.loop(1, NL)
        def _(s):
            j = lax.rem(me + s, NL)
            pltpu.make_async_remote_copy(
                src_ref=src.at[j],
                dst_ref=dst.at[me],
                send_sem=snd,
                recv_sem=rcv,
                device_id=(j, x),
                device_id_type=MESH,
            ).start()

        pltpu.make_async_copy(src.at[me], dst.at[me], rcv).start()

    def ch_send(src, dst, snd, rcv):
        for s in (2, 1, 3):
            i = lax.rem(x + s, NX)
            pltpu.make_async_remote_copy(
                src_ref=src.at[i],
                dst_ref=dst.at[x],
                send_sem=snd,
                recv_sem=rcv,
                device_id=(me, i),
                device_id_type=MESH,
            ).start()
        pltpu.make_async_copy(src.at[x], dst.at[x], rcv).start()

    def take(ref, sem):
        pltpu.make_async_copy(ref, ref, sem).wait()

    order = lax.broadcasted_iota(jnp.int32, (MODES, MODES), 0)
    place = lax.broadcasted_iota(jnp.int32, (MODES, MODES), 1)
    moved = jnp.where(order == ROWS * (place % NL) + place // NL, 1.0, 0.0).astype(BF)
    hot = dot(jnp.where(morder[...].reshape(1, MODES) == order, 1.0, 0.0).astype(BF), moved)
    pick = hot.T.astype(BF)

    loads[0].wait()
    loads[1].wait()
    for kp in range(KP):
        rows = pick[kp * 2 * NL : (kp + 1) * 2 * NL]
        table = jnp.concatenate(
            [dot(rows, tw_v[0]).astype(BF), dot(rows, tw_v[1]).astype(BF)], axis=0
        )
        for p in range(CYC // 2):
            res = dot(table, jnp.concatenate([grid_v[2 * p], grid_v[2 * p + 1]], axis=1))
            for reim in range(2):
                for k2 in range(2):
                    at = (reim * 2 + k2) * NL
                    for c in range(2):
                        row = k2 * NL * 16 + reim * 8 + 2 * p + c
                        stage[pl.ds(row, NL, stride=16), :] = res[
                            at : at + NL, c * CB : (c + 1) * CB
                        ]
        for k2 in range(2):
            part = stage[k2 * NL * 16 : (k2 + 1) * NL * 16]
            sbuf[2 * kp + k2] = part.astype(BF).reshape(NL, 16, CB)
        if kp == 0:
            pl.semaphore_wait(barrier, NL - 1 + NX - 1)
        for k in (2 * kp, 2 * kp + 1):
            lat_send(sbuf.at[k], rbuf.at[k], s_snd.at[k], s_rcv.at[k])

    loads[2].wait()
    for k in range(ROWS):
        values = leg_v[k]
        legt[k] = values.T
        leg_v[k] = (values.astype(F32) * quad[...]).astype(BF)
    loads[3].wait()
    loads[4].wait()
    for xs in range(NX):
        for xd in range(NX):
            re = mr_v[xs * CB : (xs + 1) * CB, xd * CB : (xd + 1) * CB]
            im = mi_v[xs * CB : (xs + 1) * CB, xd * CB : (xd + 1) * CB]
            r0, c0 = xs * 2 * CB, xd * 2 * CB
            wm[r0 : r0 + CB, c0 : c0 + CB] = re
            wm[r0 : r0 + CB, c0 + CB : c0 + 2 * CB] = im
            wm[r0 + CB : r0 + 2 * CB, c0 : c0 + CB] = -im
            wm[r0 + CB : r0 + 2 * CB, c0 + CB : c0 + 2 * CB] = re
    loads[5].wait()
    hot = (hot * jnp.where(order == 0, 1.0, 2.0)).astype(BF)
    for reim in range(2):
        itab[:, reim * MODES : (reim + 1) * MODES] = dot(twt_v[reim], hot).astype(BF)
    loads[6].wait()

    sub = lax.broadcasted_iota(jnp.int32, (NL, 8, CB), 1)

    def analyse(k):
        got = rbuf[k].astype(F32)
        spec = jnp.concatenate(
            [
                got[:, :8, :].reshape(NL * 8, CB).astype(BF),
                got[:, 8:, :].reshape(NL * 8, CB).astype(BF),
            ],
            axis=1,
        )
        cs[k] = dot(leg_v[k], spec).astype(BF).reshape(NX, LB, 2 * CB)
        ch_send(cs.at[k], cr.at[k], c_snd.at[k], c_rcv.at[k])

    def mix(k):
        take(cr.at[k], c_rcv.at[k])
        res = dot(jnp.concatenate([cr[k, i] for i in range(NX)], axis=1), wm[...])
        for i in range(NX):
            part = gain_v[:, i * CB : (i + 1) * CB]
            part = jnp.concatenate([part, part], axis=1)
            fs[k, i] = (res[:, i * 2 * CB : (i + 1) * 2 * CB] * part).astype(BF)
        ch_send(fs.at[k], fr.at[k], f_snd.at[k], f_rcv.at[k])

    def synthesise(k):
        take(fr.at[k], f_rcv.at[k])
        back = dot(legt[k], fr[k].reshape(MODES, 2 * CB))
        return back[:, :CB].reshape(NL, 8, CB), back[:, CB:].reshape(NL, 8, CB)

    def gather(parts, first, n):
        out = None
        for i, part in enumerate(parts):
            turned = pltpu.roll(part, (n * i - first) % 8, 1)
            out = turned if out is None else jnp.where(sub < n * i, out, turned)
        return out

    def pack_quarters(backs):
        for g in range(4):
            tiles = [
                gather([*backs[2 * i], *backs[2 * i + 1]], 2 * g, 2) for i in range(2)
            ]
            eq[g] = jnp.concatenate(tiles, axis=1).astype(BF)

    def pack_halves(backs):
        for h in range(2):
            tiles = [gather(backs[i], 4 * h, 4) for i in range(2)]
            eh[h] = jnp.concatenate(tiles, axis=1).astype(BF)

    def send_quarter(g):
        lat_send(eq.at[g], rq.at[g], q_snd.at[g], q_rcv.at[g])

    def send_half(h):
        lat_send(eh.at[h], rh.at[h], h_snd.at[h], h_rcv.at[h])

    def waves(p):
        take(rq.at[p], q_rcv.at[p])
        if p % 2 == 0:
            take(rh.at[p // 2], h_rcv.at[p // 2])
        xst[: NL * 16] = rq[p].astype(F32).reshape(NL * 16, CB)
        xst[NL * 16 :] = rh[p // 2].astype(F32).reshape(NL * 16, CB)
        cols = []
        for c in range(2):
            part = []
            for reim in range(2):
                for k in range(4):
                    part.append(xst[pl.ds(k * 4 + reim * 2 + c, NL, stride=16), :])
                for k in range(2):
                    at = NL * 16 + k * 8 + reim * 4 + 2 * (p % 2) + c
                    part.append(xst[pl.ds(at, NL, stride=16), :])
            cols.append(jnp.concatenate(part, axis=0).astype(BF))
        wave = dot(itab[...], jnp.concatenate(cols, axis=1))
        both = [grid_v[2 * p + c].astype(F32) + wave[:, c * CB : (c + 1) * CB] for c in range(2)]
        for i in range(NX):
            gs[p, i] = jnp.concatenate(
                [b[i * LON : (i + 1) * LON] for b in both], axis=0
            ).astype(BF)
        for t, (pair, at, n) in enumerate(PIECES):
            if pair == p:
                part = pl.ds(at, n)
                ch_send(
                    gs.at[p, :, part], gr.at[p, :, part], g_snd.at[t], g_rcv.at[t]
                )


    def points(t):
        p, at, n = PIECES[t]
        part = pl.ds(at, n)
        take(gr.at[p, :, part], g_rcv.at[t])
        rows = jnp.concatenate([gr[p, i, part, :] for i in range(NX)], axis=1)
        ov[p, part, :] = point_layer(rows, lng, win_v, bias, wout_v)
        copy = pltpu.make_async_copy(ov.at[p, part], out_h.at[p, part], o_sem.at[t])
        copy.start()
        return copy

    backs = []
    for k in range(ROWS):
        take(rbuf.at[k], s_rcv.at[k])
        analyse(k)
        if k >= 1:
            mix(k - 1)
        if k >= 2:
            backs.append(synthesise(k - 2))
    pack_quarters(backs)
    send_quarter(0)
    send_quarter(1)
    mix(ROWS - 1)
    backs.append(synthesise(ROWS - 2))
    backs.append(synthesise(ROWS - 1))
    pack_halves(backs[4:])
    send_half(0)
    send_half(1)
    send_quarter(2)
    send_quarter(3)
    loads[7].wait()
    loads[8].wait()
    waves(0)
    waves(1)
    copies = [points(0)]
    waves(2)
    waves(3)
    copies += [points(t) for t in range(1, len(PIECES))]

    for k in range(ROWS):
        take(sbuf.at[k, pl.ds(0, NL - 1)], s_snd.at[k])
        take(cs.at[k, pl.ds(0, NX - 1)], c_snd.at[k])
        take(fs.at[k, pl.ds(0, NX - 1)], f_snd.at[k])
    for g in range(4):
        take(eq.at[g, pl.ds(0, NL - 1)], q_snd.at[g])
    for h in range(2):
        take(eh.at[h, pl.ds(0, NL - 1)], h_snd.at[h])
    for t, (p, at, n) in enumerate(PIECES):
        part = pl.ds(at, n)
        take(gs.at[p, pl.ds(0, NX - 1), part], g_snd.at[t])
    for copy in copies:
        copy.wait()


def body(
    grid,
    legendre,
    m_order,
    quad_weights,
    mix_real,
    mix_imag,
    spec_gain,
    ln_gain,
    mlp_in,
    mlp_bias,
    mlp_out,
):
    table = twiddles()
    vm = pl.BlockSpec(memory_space=pltpu.VMEM)
    hbm = pl.BlockSpec(memory_space=pl.ANY)
    dma = pltpu.SemaphoreType.DMA
    part = pl.pallas_call(
        kernel,
        out_shape=jax.ShapeDtypeStruct((CYC // 2, 2 * LON, NX * CB), BF),
        in_specs=[vm] * 4 + [hbm] * 9,
        out_specs=hbm,
        scratch_shapes=[
            pltpu.VMEM((CYC, NLON, CB), BF),
            pltpu.VMEM((2, MODES, NLON), BF),
            pltpu.VMEM((2, NLON, MODES), BF),
            pltpu.VMEM((ROWS, MODES, NL * CYC), BF),
            pltpu.VMEM((ROWS, NL * CYC, MODES), BF),
            pltpu.VMEM(mix_real.shape, BF),
            pltpu.VMEM(mix_imag.shape, BF),
            pltpu.VMEM((LB, NX * CB), F32),
            pltpu.VMEM(mlp_in.shape, BF),
            pltpu.VMEM(mlp_out.shape, BF),
            pltpu.VMEM((NL * 32, CB), F32),
            pltpu.VMEM((ROWS, NL, 16, CB), BF),
            pltpu.VMEM((ROWS, NL, 16, CB), BF),
            pltpu.VMEM((ROWS, NX, LB, 2 * CB), BF),
            pltpu.VMEM((ROWS, NX, LB, 2 * CB), BF),
            pltpu.VMEM((2 * NX * CB, 2 * NX * CB), BF),
            pltpu.VMEM((ROWS, NX, LB, 2 * CB), BF),
            pltpu.VMEM((ROWS, NX, LB, 2 * CB), BF),
            pltpu.VMEM((4, NL, 16, CB), BF),
            pltpu.VMEM((4, NL, 16, CB), BF),
            pltpu.VMEM((2, NL, 16, CB), BF),
            pltpu.VMEM((2, NL, 16, CB), BF),
            pltpu.VMEM((NLON, 2 * MODES), BF),
            pltpu.VMEM((2 * NL * 16, CB), F32),
            pltpu.VMEM((CYC // 2, NX, 2 * LON, CB), BF),
            pltpu.VMEM((CYC // 2, NX, 2 * LON, CB), BF),
            pltpu.VMEM((CYC // 2, 2 * LON, NX * CB), BF),
            dma((9,)),
            dma((ROWS,)),
            dma((ROWS,)),
            dma((ROWS,)),
            dma((ROWS,)),
            dma((ROWS,)),
            dma((ROWS,)),
            dma((4,)),
            dma((4,)),
            dma((2,)),
            dma((2,)),
            dma((len(PIECES),)),
            dma((len(PIECES),)),
            dma((len(PIECES),)),
        ],
        compiler_params=pltpu.CompilerParams(
            collective_id=0, has_side_effects=True, vmem_limit_bytes=60 << 20
        ),
        name="sfno_block",
    )(
        m_order,
        quad_weights[None, :],
        ln_gain[None, :],
        mlp_bias[None, :],
        grid,
        jnp.asarray(table),
        jnp.asarray(np.ascontiguousarray(table.transpose(0, 2, 1))),
        legendre,
        mix_real,
        mix_imag,
        spec_gain,
        mlp_in,
        mlp_out,
    )
    out = pl.pallas_call(
        finish,
        out_shape=jax.ShapeDtypeStruct(part.shape, BF),
        in_specs=[hbm],
        out_specs=hbm,
        scratch_shapes=[
            pltpu.VMEM(part.shape, BF),
            dma((CYC // 2,)),
            dma((CYC // 2,)),
        ],
        compiler_params=pltpu.CompilerParams(vmem_limit_bytes=60 << 20),
        name="move_result",
    )(part)
    return out.reshape(CYC, LON, NX * CB)


def solution(mesh):
    placed = (P("lat", None, "ch"), P("lat", None, None)) + (P(),) * 9
    return jax.shard_map(
        body, mesh=mesh, in_specs=placed, out_specs=P("lat", "ch", None), check_vma=False
    )
```

```python
import math

import jax
import jax.numpy as jnp
import numpy as np
import ml_dtypes
from jax import lax
from jax.experimental import pallas as pl
from jax.experimental.pallas import tpu as pltpu
from jax.sharding import PartitionSpec as P

NLON = 1440
MODES = 384
NL = 64
NX = 4
CYC = 8
ROWS = 6
CB = 128
LB = MODES // NX
LQ = NL // NX
LON = NLON // NX
KP = ROWS // 2
PIECES = [(0, 0, 720), (1, 0, 720), (2, 0, 720), (3, 0, 256), (3, 256, 256), (3, 512, 208)]
MESH = pl.DeviceIdType.MESH
BF = jnp.bfloat16
F32 = jnp.float32


def twiddles():
    index = np.arange(MODES)[:, None] * np.arange(NLON)[None, :] % NLON
    angle = index * (2.0 * math.pi / NLON)
    table = np.stack([np.cos(angle), -np.sin(angle)]) / math.sqrt(NLON)
    return table.astype(np.float32).astype(ml_dtypes.bfloat16)


def dot(a, b):
    return jnp.dot(a, b, preferred_element_type=F32)


def point_layer(rows, lng, win, bias, wout):
    values = rows.astype(F32)
    center = jnp.mean(values, axis=-1, keepdims=True)
    moved = values - center
    spread = jnp.mean(moved * moved, axis=-1, keepdims=True)
    normed = (moved * lax.rsqrt(spread + 1e-05) * lng[...]).astype(BF)
    inner = dot(normed, win[...]) + bias[...]
    half = 0.5 * inner
    root = math.sqrt(2.0 / math.pi)
    bent = jnp.tanh(inner * (root + (root * 0.044715) * (inner * inner)))
    hidden = (half + half * bent).astype(BF)
    return (values + dot(hidden, wout[...])).astype(BF)


def finish(part_h, out_h, hold, i_sem, o_sem):
    pairs = range(CYC // 2)
    into = [pltpu.make_async_copy(part_h.at[p], hold.at[p], i_sem.at[p]) for p in pairs]
    out = [pltpu.make_async_copy(hold.at[p], out_h.at[p], o_sem.at[p]) for p in pairs]
    for copy in into:
        copy.start()
    for p in pairs:
        into[p].wait()
        out[p].start()
    for copy in out:
        copy.wait()


def kernel(
    morder,
    quad,
    lng,
    bias,
    grid_h,
    tw_h,
    twt_h,
    leg_h,
    mr_h,
    mi_h,
    gain_h,
    win_h,
    wout_h,
    out_h,
    grid_v,
    tw_v,
    twt_v,
    leg_v,
    legt,
    mr_v,
    mi_v,
    gain_v,
    gaind_v,
    win_v,
    wout_v,
    stage,
    sbuf,
    rbuf,
    mr_in,
    mr_out,
    sb2,
    cs,
    cr,
    wm,
    fs,
    fr,
    eq,
    rq,
    eh,
    rh,
    itab,
    xst,
    gs,
    gr,
    ov,
    load_sem,
    s_snd,
    s_rcv,
    m_snd,
    m_rcv,
    c_snd,
    c_rcv,
    f_snd,
    f_rcv,
    q_snd,
    q_rcv,
    h_snd,
    h_rcv,
    g_snd,
    g_rcv,
    o_sem,
):
    me = lax.axis_index("lat")
    x = lax.axis_index("ch")

    loads = [
        pltpu.make_async_copy(src, dst, load_sem.at[i])
        for i, (src, dst) in enumerate(
            [
                (tw_h, tw_v),
                (grid_h, grid_v),
                (mr_h, mr_v),
                (mi_h, mi_v),
                (leg_h, leg_v),
                (twt_h, twt_v),
                (gain_h.at[pl.ds(pl.multiple_of(x * LB, LB), LB)], gain_v),
                (gain_h.at[:, pl.ds(pl.multiple_of(x * CB, CB), CB)], gaind_v),
                (win_h, win_v),
                (wout_h, wout_v),
            ]
        )
    ]
    for load in loads:
        load.start()

    barrier = pltpu.get_barrier_semaphore()

    @pl.loop(1, NL)
    def _(s):
        pl.semaphore_signal(
            barrier, inc=1, device_id=(lax.rem(me + s, NL), x), device_id_type=MESH
        )

    for s in range(1, NX):
        pl.semaphore_signal(
            barrier, inc=1, device_id=(me, lax.rem(x + s, NX)), device_id_type=MESH
        )

    def lat_send(src, dst, snd, rcv):
        @pl.loop(1, NL)
        def _(s):
            j = lax.rem(me + s, NL)
            pltpu.make_async_remote_copy(
                src_ref=src.at[j],
                dst_ref=dst.at[me],
                send_sem=snd,
                recv_sem=rcv,
                device_id=(j, x),
                device_id_type=MESH,
            ).start()

        pltpu.make_async_copy(src.at[me], dst.at[me], rcv).start()

    def ch_send(src, dst, snd, rcv):
        for s in (2, 1, 3):
            i = lax.rem(x + s, NX)
            pltpu.make_async_remote_copy(
                src_ref=src(i),
                dst_ref=dst,
                send_sem=snd,
                recv_sem=rcv,
                device_id=(me, i),
                device_id_type=MESH,
            ).start()
        pltpu.make_async_copy(src(x), dst, rcv).start()

    def take(ref, sem):
        pltpu.make_async_copy(ref, ref, sem).wait()

    order = lax.broadcasted_iota(jnp.int32, (MODES, MODES), 0)
    place = lax.broadcasted_iota(jnp.int32, (MODES, MODES), 1)
    moved = jnp.where(order == ROWS * (place % NL) + place // NL, 1.0, 0.0).astype(BF)
    hot = dot(jnp.where(morder[...].reshape(1, MODES) == order, 1.0, 0.0).astype(BF), moved)
    pick = hot.T.astype(BF)

    loads[0].wait()
    loads[1].wait()

    def fourier(kp):
        rows = pick[kp * 2 * NL : (kp + 1) * 2 * NL]
        table = jnp.concatenate(
            [dot(rows, tw_v[0]).astype(BF), dot(rows, tw_v[1]).astype(BF)], axis=0
        )
        for p in range(CYC // 2):
            res = dot(table, jnp.concatenate([grid_v[2 * p], grid_v[2 * p + 1]], axis=1))
            for reim in range(2):
                for k2 in range(2):
                    at = (reim * 2 + k2) * NL
                    for c in range(2):
                        row = k2 * NL * 16 + reim * 8 + 2 * p + c
                        stage[pl.ds(row, NL, stride=16), :] = res[
                            at : at + NL, c * CB : (c + 1) * CB
                        ]
        for k2 in range(2):
            part = stage[k2 * NL * 16 : (k2 + 1) * NL * 16]
            sbuf[2 * kp + k2] = part.astype(BF).reshape(NL, 16, CB)

    def spectra_send(src, k):
        lat_send(src, rbuf.at[k], s_snd.at[k], s_rcv.at[k])

    def split(tiles):
        tiles = tiles.astype(F32)
        n = tiles.shape[0] * 8
        return [tiles[:, i * 8 : (i + 1) * 8, :].reshape(n, CB).astype(BF) for i in range(2)]

    fourier(0)
    pl.semaphore_wait(barrier, NL - 1 + NX - 1)
    spectra_send(sbuf.at[0], 0)
    spectra_send(sbuf.at[1], 1)

    fourier(2)
    ch_send(
        lambda i: sbuf.at[pl.ds(4, 2), pl.ds(i * LQ, LQ)], mr_in.at[x], m_snd.at[0], m_rcv.at[0]
    )
    loads[2].wait()
    loads[3].wait()
    for xs in range(NX):
        for xd in range(NX):
            re = mr_v[xs * CB : (xs + 1) * CB, xd * CB : (xd + 1) * CB]
            im = mi_v[xs * CB : (xs + 1) * CB, xd * CB : (xd + 1) * CB]
            r0, c0 = xs * 2 * CB, xd * 2 * CB
            wm[r0 : r0 + CB, c0 : c0 + CB] = re
            wm[r0 : r0 + CB, c0 + CB : c0 + 2 * CB] = im
            wm[r0 + CB : r0 + 2 * CB, c0 : c0 + CB] = -im
            wm[r0 + CB : r0 + 2 * CB, c0 + CB : c0 + 2 * CB] = re
    fourier(1)
    spectra_send(sbuf.at[2], 2)
    spectra_send(sbuf.at[3], 3)

    take(mr_in, m_rcv.at[0])
    lhs = []
    for i in range(NX):
        lhs += split(mr_in[i].reshape(2 * LQ, 16, CB))
    res = dot(jnp.concatenate(lhs, axis=1), wm[...])
    for i in range(NX):
        part = [
            res[:, (2 * i + reim) * CB : (2 * i + reim + 1) * CB].reshape(2 * LQ, 8, CB)
            for reim in range(2)
        ]
        mr_out[i] = jnp.concatenate(part, axis=1).astype(BF).reshape(2, LQ, 16, CB)
    ch_send(lambda i: mr_out.at[i], sb2.at[:, pl.ds(x * LQ, LQ)], m_snd.at[1], m_rcv.at[1])

    loads[4].wait()
    for k in range(ROWS):
        values = leg_v[k]
        legt[k] = values.T
        leg_v[k] = (values.astype(F32) * quad[...]).astype(BF)
    loads[5].wait()
    hot = (hot * jnp.where(order == 0, 1.0, 2.0)).astype(BF)
    for reim in range(2):
        itab[:, reim * MODES : (reim + 1) * MODES] = dot(twt_v[reim], hot).astype(BF)
    loads[6].wait()
    loads[7].wait()

    sub = lax.broadcasted_iota(jnp.int32, (NL, 8, CB), 1)

    def analyse(k):
        take(rbuf.at[k], s_rcv.at[k])
        return dot(leg_v[k], jnp.concatenate(split(rbuf[k]), axis=1))

    def offer(k):
        cs[k] = analyse(k).astype(BF).reshape(NX, LB, 2 * CB)
        ch_send(lambda i: cs.at[k, i], cr.at[k, x], c_snd.at[k], c_rcv.at[k])

    def mix(k):
        take(cr.at[k], c_rcv.at[k])
        res = dot(jnp.concatenate([cr[k, i] for i in range(NX)], axis=1), wm[...])
        for i in range(NX):
            part = gain_v[:, i * CB : (i + 1) * CB]
            part = jnp.concatenate([part, part], axis=1)
            fs[k, i] = (res[:, i * 2 * CB : (i + 1) * 2 * CB] * part).astype(BF)
        ch_send(lambda i: fs.at[k, i], fr.at[k, x], f_snd.at[k], f_rcv.at[k])

    def synthesise(k, filt):
        back = dot(legt[k], filt)
        return back[:, :CB].reshape(NL, 8, CB), back[:, CB:].reshape(NL, 8, CB)

    def received(k):
        take(fr.at[k], f_rcv.at[k])
        return fr[k].reshape(MODES, 2 * CB)

    def filtered(k):
        gain = gaind_v[...]
        return (analyse(k) * jnp.concatenate([gain, gain], axis=1)).astype(BF)

    def gather(parts, first, n):
        out = None
        for i, part in enumerate(parts):
            turned = pltpu.roll(part, (n * i - first) % 8, 1)
            out = turned if out is None else jnp.where(sub < n * i, out, turned)
        return out

    def pack_quarters(backs):
        for g in range(4):
            tiles = [
                gather([*backs[2 * i], *backs[2 * i + 1]], 2 * g, 2) for i in range(2)
            ]
            eq[g] = jnp.concatenate(tiles, axis=1).astype(BF)

    def pack_halves(backs):
        for h in range(2):
            tiles = [gather(backs[i], 4 * h, 4) for i in range(2)]
            eh[h] = jnp.concatenate(tiles, axis=1).astype(BF)

    def send_quarter(g):
        lat_send(eq.at[g], rq.at[g], q_snd.at[g], q_rcv.at[g])

    def send_half(h):
        lat_send(eh.at[h], rh.at[h], h_snd.at[h], h_rcv.at[h])

    def waves(p):
        take(rq.at[p], q_rcv.at[p])
        if p % 2 == 0:
            take(rh.at[p // 2], h_rcv.at[p // 2])
        xst[: NL * 16] = rq[p].astype(F32).reshape(NL * 16, CB)
        xst[NL * 16 :] = rh[p // 2].astype(F32).reshape(NL * 16, CB)
        cols = []
        for c in range(2):
            part = []
            for reim in range(2):
                for k in range(4):
                    part.append(xst[pl.ds(k * 4 + reim * 2 + c, NL, stride=16), :])
                for k in range(2):
                    at = NL * 16 + k * 8 + reim * 4 + 2 * (p % 2) + c
                    part.append(xst[pl.ds(at, NL, stride=16), :])
            cols.append(jnp.concatenate(part, axis=0).astype(BF))
        wave = dot(itab[...], jnp.concatenate(cols, axis=1))
        both = [grid_v[2 * p + c].astype(F32) + wave[:, c * CB : (c + 1) * CB] for c in range(2)]
        for i in range(NX):
            gs[p, i] = jnp.concatenate(
                [b[i * LON : (i + 1) * LON] for b in both], axis=0
            ).astype(BF)
        for t, (pair, at, n) in enumerate(PIECES):
            if pair == p:
                part = pl.ds(at, n)
                ch_send(
                    lambda i: gs.at[p, i, part], gr.at[p, x, part], g_snd.at[t], g_rcv.at[t]
                )


    def points(t):
        p, at, n = PIECES[t]
        part = pl.ds(at, n)
        take(gr.at[p, :, part], g_rcv.at[t])
        rows = jnp.concatenate([gr[p, i, part, :] for i in range(NX)], axis=1)
        ov[p, part, :] = point_layer(rows, lng, win_v, bias, wout_v)
        copy = pltpu.make_async_copy(ov.at[p, part], out_h.at[p, part], o_sem.at[t])
        copy.start()
        return copy

    offer(0)
    offer(1)
    mix(0)
    take(sb2, m_rcv.at[1])
    spectra_send(sb2.at[0], 4)
    spectra_send(sb2.at[1], 5)
    offer(2)
    mix(1)
    backs = [synthesise(0, received(0))]
    offer(3)
    mix(2)
    backs.append(synthesise(1, received(1)))
    backs.append(synthesise(2, received(2)))
    mix(3)
    backs.append(synthesise(3, received(3)))
    pack_quarters(backs)
    send_quarter(0)
    pack_halves([synthesise(k, filtered(k)) for k in (4, 5)])
    send_half(0)
    send_quarter(1)
    send_half(1)
    send_quarter(2)
    send_quarter(3)
    loads[8].wait()
    loads[9].wait()
    waves(0)
    waves(1)
    copies = [points(0)]
    waves(2)
    waves(3)
    copies += [points(t) for t in range(1, len(PIECES))]

    for k in range(ROWS):
        take(sbuf.at[k, pl.ds(0, NL - 1)], s_snd.at[k])
    for k in range(4):
        take(cs.at[k, pl.ds(0, NX - 1)], c_snd.at[k])
        take(fs.at[k, pl.ds(0, NX - 1)], f_snd.at[k])
    for i in range(2):
        take(mr_out.at[pl.ds(0, NX - 1)], m_snd.at[i])
    for g in range(4):
        take(eq.at[g, pl.ds(0, NL - 1)], q_snd.at[g])
    for h in range(2):
        take(eh.at[h, pl.ds(0, NL - 1)], h_snd.at[h])
    for t, (p, at, n) in enumerate(PIECES):
        part = pl.ds(at, n)
        take(gs.at[p, pl.ds(0, NX - 1), part], g_snd.at[t])
    for copy in copies:
        copy.wait()


def body(
    grid,
    legendre,
    m_order,
    quad_weights,
    mix_real,
    mix_imag,
    spec_gain,
    ln_gain,
    mlp_in,
    mlp_bias,
    mlp_out,
):
    table = twiddles()
    vm = pl.BlockSpec(memory_space=pltpu.VMEM)
    hbm = pl.BlockSpec(memory_space=pl.ANY)
    dma = pltpu.SemaphoreType.DMA
    part = pl.pallas_call(
        kernel,
        out_shape=jax.ShapeDtypeStruct((CYC // 2, 2 * LON, NX * CB), BF),
        in_specs=[vm] * 4 + [hbm] * 9,
        out_specs=hbm,
        scratch_shapes=[
            pltpu.VMEM((CYC, NLON, CB), BF),
            pltpu.VMEM((2, MODES, NLON), BF),
            pltpu.VMEM((2, NLON, MODES), BF),
            pltpu.VMEM((ROWS, MODES, NL * CYC), BF),
            pltpu.VMEM((ROWS, NL * CYC, MODES), BF),
            pltpu.VMEM(mix_real.shape, BF),
            pltpu.VMEM(mix_imag.shape, BF),
            pltpu.VMEM((LB, NX * CB), F32),
            pltpu.VMEM((MODES, CB), F32),
            pltpu.VMEM(mlp_in.shape, BF),
            pltpu.VMEM(mlp_out.shape, BF),
            pltpu.VMEM((NL * 32, CB), F32),
            pltpu.VMEM((ROWS, NL, 16, CB), BF),
            pltpu.VMEM((ROWS, NL, 16, CB), BF),
            pltpu.VMEM((NX, 2, LQ, 16, CB), BF),
            pltpu.VMEM((NX, 2, LQ, 16, CB), BF),
            pltpu.VMEM((2, NL, 16, CB), BF),
            pltpu.VMEM((4, NX, LB, 2 * CB), BF),
            pltpu.VMEM((4, NX, LB, 2 * CB), BF),
            pltpu.VMEM((2 * NX * CB, 2 * NX * CB), BF),
            pltpu.VMEM((4, NX, LB, 2 * CB), BF),
            pltpu.VMEM((4, NX, LB, 2 * CB), BF),
            pltpu.VMEM((4, NL, 16, CB), BF),
            pltpu.VMEM((4, NL, 16, CB), BF),
            pltpu.VMEM((2, NL, 16, CB), BF),
            pltpu.VMEM((2, NL, 16, CB), BF),
            pltpu.VMEM((NLON, 2 * MODES), BF),
            pltpu.VMEM((2 * NL * 16, CB), F32),
            pltpu.VMEM((CYC // 2, NX, 2 * LON, CB), BF),
            pltpu.VMEM((CYC // 2, NX, 2 * LON, CB), BF),
            pltpu.VMEM((CYC // 2, 2 * LON, NX * CB), BF),
            dma((10,)),
            dma((ROWS,)),
            dma((ROWS,)),
            dma((2,)),
            dma((2,)),
            dma((4,)),
            dma((4,)),
            dma((4,)),
            dma((4,)),
            dma((4,)),
            dma((4,)),
            dma((2,)),
            dma((2,)),
            dma((len(PIECES),)),
            dma((len(PIECES),)),
            dma((len(PIECES),)),
        ],
        compiler_params=pltpu.CompilerParams(
            collective_id=0, has_side_effects=True, vmem_limit_bytes=60 << 20
        ),
        name="sfno_block",
    )(
        m_order,
        quad_weights[None, :],
        ln_gain[None, :],
        mlp_bias[None, :],
        grid,
        jnp.asarray(table),
        jnp.asarray(np.ascontiguousarray(table.transpose(0, 2, 1))),
        legendre,
        mix_real,
        mix_imag,
        spec_gain,
        mlp_in,
        mlp_out,
    )
    out = pl.pallas_call(
        finish,
        out_shape=jax.ShapeDtypeStruct(part.shape, BF),
        in_specs=[hbm],
        out_specs=hbm,
        scratch_shapes=[
            pltpu.VMEM(part.shape, BF),
            dma((CYC // 2,)),
            dma((CYC // 2,)),
        ],
        compiler_params=pltpu.CompilerParams(vmem_limit_bytes=60 << 20),
        name="move_result",
    )(part)
    return out.reshape(CYC, LON, NX * CB)


def solution(mesh):
    placed = (P("lat", None, "ch"), P("lat", None, None)) + (P(),) * 9
    return jax.shard_map(
        body, mesh=mesh, in_specs=placed, out_specs=P("lat", "ch", None), check_vma=False
    )
```

```python
import math

import jax
import jax.numpy as jnp
import numpy as np
import ml_dtypes
from jax import lax
from jax.experimental import pallas as pl
from jax.experimental.pallas import tpu as pltpu
from jax.sharding import PartitionSpec as P

NLON = 1440
MODES = 384
NL = 64
NX = 4
CYC = 8
ROWS = 6
CB = 128
LB = MODES // NX
LQ = NL // NX
LON = NLON // NX
KP = ROWS // 2
PIECES = [(0, 0, 720), (1, 0, 720), (2, 0, 720), (3, 0, 256), (3, 256, 256), (3, 512, 208)]
MESH = pl.DeviceIdType.MESH
BF = jnp.bfloat16
F32 = jnp.float32


def twiddles():
    index = np.arange(MODES)[:, None] * np.arange(NLON)[None, :] % NLON
    angle = index * (2.0 * math.pi / NLON)
    table = np.stack([np.cos(angle), -np.sin(angle)]) / math.sqrt(NLON)
    return table.astype(np.float32).astype(ml_dtypes.bfloat16)


def dot(a, b):
    return jnp.dot(a, b, preferred_element_type=F32)


def point_layer(rows, lng, win, bias, wout):
    values = rows.astype(F32)
    center = jnp.mean(values, axis=-1, keepdims=True)
    moved = values - center
    spread = jnp.mean(moved * moved, axis=-1, keepdims=True)
    normed = (moved * lax.rsqrt(spread + 1e-05) * lng[...]).astype(BF)
    inner = dot(normed, win[...]) + bias[...]
    half = 0.5 * inner
    root = math.sqrt(2.0 / math.pi)
    bent = jnp.tanh(inner * (root + (root * 0.044715) * (inner * inner)))
    hidden = (half + half * bent).astype(BF)
    return (values + dot(hidden, wout[...])).astype(BF)


def finish(part_h, out_h, hold, i_sem, o_sem):
    pairs = range(CYC // 2)
    into = [pltpu.make_async_copy(part_h.at[p], hold.at[p], i_sem.at[p]) for p in pairs]
    out = [pltpu.make_async_copy(hold.at[p], out_h.at[p], o_sem.at[p]) for p in pairs]
    for copy in into:
        copy.start()
    for p in pairs:
        into[p].wait()
        out[p].start()
    for copy in out:
        copy.wait()


def kernel(
    morder,
    quad,
    lng,
    bias,
    grid_h,
    tw_h,
    twt_h,
    leg_h,
    mr_h,
    mi_h,
    gain_h,
    win_h,
    wout_h,
    out_h,
    grid_v,
    tw_v,
    twt_v,
    leg_v,
    legt,
    mr_v,
    mi_v,
    gain_v,
    gaind_v,
    win_v,
    wout_v,
    stage,
    sbuf,
    rbuf,
    mr_in,
    mr_out,
    sb2,
    cs,
    cr,
    wm,
    fs,
    fr,
    eq,
    rq,
    eh,
    rh,
    itab,
    xst,
    gs,
    gr,
    ov,
    load_sem,
    s_snd,
    s_rcv,
    m_snd,
    m_rcv,
    c_snd,
    c_rcv,
    f_snd,
    f_rcv,
    q_snd,
    q_rcv,
    h_snd,
    h_rcv,
    g_snd,
    g_rcv,
    o_sem,
):
    me = lax.axis_index("lat")
    x = lax.axis_index("ch")

    loads = [
        pltpu.make_async_copy(src, dst, load_sem.at[i])
        for i, (src, dst) in enumerate(
            [
                (tw_h, tw_v),
                (grid_h, grid_v),
                (mr_h, mr_v),
                (mi_h, mi_v),
                (leg_h, leg_v),
                (twt_h, twt_v),
                (gain_h.at[pl.ds(pl.multiple_of(x * LB, LB), LB)], gain_v),
                (gain_h.at[:, pl.ds(pl.multiple_of(x * CB, CB), CB)], gaind_v),
                (win_h, win_v),
                (wout_h, wout_v),
            ]
        )
    ]
    for load in loads:
        load.start()

    barrier = pltpu.get_barrier_semaphore()

    @pl.loop(1, NL)
    def _(s):
        pl.semaphore_signal(
            barrier, inc=1, device_id=(lax.rem(me + s, NL), x), device_id_type=MESH
        )

    for s in range(1, NX):
        pl.semaphore_signal(
            barrier, inc=1, device_id=(me, lax.rem(x + s, NX)), device_id_type=MESH
        )

    def lat_send(src, dst, snd, rcv):
        @pl.loop(1, NL)
        def _(s):
            j = lax.rem(me + s, NL)
            pltpu.make_async_remote_copy(
                src_ref=src.at[j],
                dst_ref=dst.at[me],
                send_sem=snd,
                recv_sem=rcv,
                device_id=(j, x),
                device_id_type=MESH,
            ).start()

        pltpu.make_async_copy(src.at[me], dst.at[me], rcv).start()

    def ch_send(src, dst, snd, rcv):
        for s in (2, 1, 3):
            i = lax.rem(x + s, NX)
            pltpu.make_async_remote_copy(
                src_ref=src(i),
                dst_ref=dst,
                send_sem=snd,
                recv_sem=rcv,
                device_id=(me, i),
                device_id_type=MESH,
            ).start()
        pltpu.make_async_copy(src(x), dst, rcv).start()

    def take(ref, sem):
        pltpu.make_async_copy(ref, ref, sem).wait()

    order = lax.broadcasted_iota(jnp.int32, (MODES, MODES), 0)
    place = lax.broadcasted_iota(jnp.int32, (MODES, MODES), 1)
    moved = jnp.where(order == ROWS * (place % NL) + place // NL, 1.0, 0.0).astype(BF)
    hot = dot(jnp.where(morder[...].reshape(1, MODES) == order, 1.0, 0.0).astype(BF), moved)
    pick = hot.T.astype(BF)

    loads[0].wait()
    loads[1].wait()

    def fourier(kp):
        rows = pick[kp * 2 * NL : (kp + 1) * 2 * NL]
        table = jnp.concatenate(
            [dot(rows, tw_v[0]).astype(BF), dot(rows, tw_v[1]).astype(BF)], axis=0
        )
        for p in range(CYC // 2):
            res = dot(table, jnp.concatenate([grid_v[2 * p], grid_v[2 * p + 1]], axis=1))
            for reim in range(2):
                for k2 in range(2):
                    at = (reim * 2 + k2) * NL
                    for c in range(2):
                        row = k2 * NL * 16 + reim * 8 + 2 * p + c
                        stage[pl.ds(row, NL, stride=16), :] = res[
                            at : at + NL, c * CB : (c + 1) * CB
                        ]
        for k2 in range(2):
            part = stage[k2 * NL * 16 : (k2 + 1) * NL * 16]
            sbuf[2 * kp + k2] = part.astype(BF).reshape(NL, 16, CB)

    def spectra_send(src, k):
        lat_send(src, rbuf.at[k], s_snd.at[k], s_rcv.at[k])

    def split(tiles):
        tiles = tiles.astype(F32)
        n = tiles.shape[0] * 8
        return [tiles[:, i * 8 : (i + 1) * 8, :].reshape(n, CB).astype(BF) for i in range(2)]

    fourier(0)
    pl.semaphore_wait(barrier, NL - 1 + NX - 1)
    spectra_send(sbuf.at[0], 0)

    fourier(2)
    ch_send(
        lambda i: sbuf.at[pl.ds(4, 2), pl.ds(i * LQ, LQ)], mr_in.at[x], m_snd.at[0], m_rcv.at[0]
    )
    spectra_send(sbuf.at[1], 1)
    loads[2].wait()
    loads[3].wait()
    for xs in range(NX):
        for xd in range(NX):
            re = mr_v[xs * CB : (xs + 1) * CB, xd * CB : (xd + 1) * CB]
            im = mi_v[xs * CB : (xs + 1) * CB, xd * CB : (xd + 1) * CB]
            r0, c0 = xs * 2 * CB, xd * 2 * CB
            wm[r0 : r0 + CB, c0 : c0 + CB] = re
            wm[r0 : r0 + CB, c0 + CB : c0 + 2 * CB] = im
            wm[r0 + CB : r0 + 2 * CB, c0 : c0 + CB] = -im
            wm[r0 + CB : r0 + 2 * CB, c0 + CB : c0 + 2 * CB] = re
    fourier(1)
    spectra_send(sbuf.at[2], 2)
    spectra_send(sbuf.at[3], 3)

    take(mr_in, m_rcv.at[0])
    lhs = []
    for i in range(NX):
        lhs += split(mr_in[i].reshape(2 * LQ, 16, CB))
    res = dot(jnp.concatenate(lhs, axis=1), wm[...])
    for i in range(NX):
        part = [
            res[:, (2 * i + reim) * CB : (2 * i + reim + 1) * CB].reshape(2 * LQ, 8, CB)
            for reim in range(2)
        ]
        mr_out[i] = jnp.concatenate(part, axis=1).astype(BF).reshape(2, LQ, 16, CB)
    ch_send(lambda i: mr_out.at[i], sb2.at[:, pl.ds(x * LQ, LQ)], m_snd.at[1], m_rcv.at[1])

    loads[4].wait()
    for k in range(ROWS):
        values = leg_v[k]
        legt[k] = values.T
        leg_v[k] = (values.astype(F32) * quad[...]).astype(BF)
    loads[5].wait()
    hot = (hot * jnp.where(order == 0, 1.0, 2.0)).astype(BF)
    for reim in range(2):
        itab[:, reim * MODES : (reim + 1) * MODES] = dot(twt_v[reim], hot).astype(BF)
    loads[6].wait()
    loads[7].wait()

    sub = lax.broadcasted_iota(jnp.int32, (NL, 8, CB), 1)

    def analyse(k):
        take(rbuf.at[k], s_rcv.at[k])
        return dot(leg_v[k], jnp.concatenate(split(rbuf[k]), axis=1))

    def offer(k):
        cs[k] = analyse(k).astype(BF).reshape(NX, LB, 2 * CB)
        ch_send(lambda i: cs.at[k, i], cr.at[k, x], c_snd.at[k], c_rcv.at[k])

    def mix(k):
        take(cr.at[k], c_rcv.at[k])
        res = dot(jnp.concatenate([cr[k, i] for i in range(NX)], axis=1), wm[...])
        for i in range(NX):
            part = gain_v[:, i * CB : (i + 1) * CB]
            part = jnp.concatenate([part, part], axis=1)
            fs[k, i] = (res[:, i * 2 * CB : (i + 1) * 2 * CB] * part).astype(BF)
        ch_send(lambda i: fs.at[k, i], fr.at[k, x], f_snd.at[k], f_rcv.at[k])

    def synthesise(k, filt):
        back = dot(legt[k], filt)
        return back[:, :CB].reshape(NL, 8, CB), back[:, CB:].reshape(NL, 8, CB)

    def received(k):
        take(fr.at[k], f_rcv.at[k])
        return fr[k].reshape(MODES, 2 * CB)

    def filtered(k):
        gain = gaind_v[...]
        return (analyse(k) * jnp.concatenate([gain, gain], axis=1)).astype(BF)

    def gather(parts, first, n):
        out = None
        for i, part in enumerate(parts):
            turned = pltpu.roll(part, (n * i - first) % 8, 1)
            out = turned if out is None else jnp.where(sub < n * i, out, turned)
        return out

    def pack_quarters(backs):
        for g in range(4):
            tiles = [
                gather([*backs[2 * i], *backs[2 * i + 1]], 2 * g, 2) for i in range(2)
            ]
            eq[g] = jnp.concatenate(tiles, axis=1).astype(BF)

    def pack_halves(backs):
        for h in range(2):
            tiles = [gather(backs[i], 4 * h, 4) for i in range(2)]
            eh[h] = jnp.concatenate(tiles, axis=1).astype(BF)

    def send_quarter(g):
        lat_send(eq.at[g], rq.at[g], q_snd.at[g], q_rcv.at[g])

    def send_half(h):
        lat_send(eh.at[h], rh.at[h], h_snd.at[h], h_rcv.at[h])

    def waves(p):
        take(rq.at[p], q_rcv.at[p])
        if p % 2 == 0:
            take(rh.at[p // 2], h_rcv.at[p // 2])
        xst[: NL * 16] = rq[p].astype(F32).reshape(NL * 16, CB)
        xst[NL * 16 :] = rh[p // 2].astype(F32).reshape(NL * 16, CB)
        cols = []
        for c in range(2):
            part = []
            for reim in range(2):
                for k in range(4):
                    part.append(xst[pl.ds(k * 4 + reim * 2 + c, NL, stride=16), :])
                for k in range(2):
                    at = NL * 16 + k * 8 + reim * 4 + 2 * (p % 2) + c
                    part.append(xst[pl.ds(at, NL, stride=16), :])
            cols.append(jnp.concatenate(part, axis=0).astype(BF))
        wave = dot(itab[...], jnp.concatenate(cols, axis=1))
        both = [grid_v[2 * p + c].astype(F32) + wave[:, c * CB : (c + 1) * CB] for c in range(2)]
        for i in range(NX):
            gs[p, i] = jnp.concatenate(
                [b[i * LON : (i + 1) * LON] for b in both], axis=0
            ).astype(BF)
        for t, (pair, at, n) in enumerate(PIECES):
            if pair == p:
                part = pl.ds(at, n)
                ch_send(
                    lambda i: gs.at[p, i, part], gr.at[p, x, part], g_snd.at[t], g_rcv.at[t]
                )


    def points(t):
        p, at, n = PIECES[t]
        part = pl.ds(at, n)
        take(gr.at[p, :, part], g_rcv.at[t])
        rows = jnp.concatenate([gr[p, i, part, :] for i in range(NX)], axis=1)
        ov[p, part, :] = point_layer(rows, lng, win_v, bias, wout_v)
        copy = pltpu.make_async_copy(ov.at[p, part], out_h.at[p, part], o_sem.at[t])
        copy.start()
        return copy

    offer(0)
    take(sb2, m_rcv.at[1])
    spectra_send(sb2.at[0], 4)
    spectra_send(sb2.at[1], 5)
    offer(1)
    mix(0)
    offer(2)
    mix(1)
    backs = [synthesise(0, received(0))]
    offer(3)
    mix(2)
    backs.append(synthesise(1, received(1)))
    backs.append(synthesise(2, received(2)))
    mix(3)
    backs.append(synthesise(3, received(3)))
    pack_quarters(backs)
    send_quarter(0)
    pack_halves([synthesise(k, filtered(k)) for k in (4, 5)])
    send_half(0)
    send_quarter(1)
    send_half(1)
    send_quarter(2)
    send_quarter(3)
    loads[8].wait()
    loads[9].wait()
    waves(0)
    waves(1)
    copies = [points(0)]
    waves(2)
    waves(3)
    copies += [points(t) for t in range(1, len(PIECES))]

    for k in range(ROWS):
        take(sbuf.at[k, pl.ds(0, NL - 1)], s_snd.at[k])
    for k in range(4):
        take(cs.at[k, pl.ds(0, NX - 1)], c_snd.at[k])
        take(fs.at[k, pl.ds(0, NX - 1)], f_snd.at[k])
    for i in range(2):
        take(mr_out.at[pl.ds(0, NX - 1)], m_snd.at[i])
    for g in range(4):
        take(eq.at[g, pl.ds(0, NL - 1)], q_snd.at[g])
    for h in range(2):
        take(eh.at[h, pl.ds(0, NL - 1)], h_snd.at[h])
    for t, (p, at, n) in enumerate(PIECES):
        part = pl.ds(at, n)
        take(gs.at[p, pl.ds(0, NX - 1), part], g_snd.at[t])
    for copy in copies:
        copy.wait()


def body(
    grid,
    legendre,
    m_order,
    quad_weights,
    mix_real,
    mix_imag,
    spec_gain,
    ln_gain,
    mlp_in,
    mlp_bias,
    mlp_out,
):
    table = twiddles()
    vm = pl.BlockSpec(memory_space=pltpu.VMEM)
    hbm = pl.BlockSpec(memory_space=pl.ANY)
    dma = pltpu.SemaphoreType.DMA
    part = pl.pallas_call(
        kernel,
        out_shape=jax.ShapeDtypeStruct((CYC // 2, 2 * LON, NX * CB), BF),
        in_specs=[vm] * 4 + [hbm] * 9,
        out_specs=hbm,
        scratch_shapes=[
            pltpu.VMEM((CYC, NLON, CB), BF),
            pltpu.VMEM((2, MODES, NLON), BF),
            pltpu.VMEM((2, NLON, MODES), BF),
            pltpu.VMEM((ROWS, MODES, NL * CYC), BF),
            pltpu.VMEM((ROWS, NL * CYC, MODES), BF),
            pltpu.VMEM(mix_real.shape, BF),
            pltpu.VMEM(mix_imag.shape, BF),
            pltpu.VMEM((LB, NX * CB), F32),
            pltpu.VMEM((MODES, CB), F32),
            pltpu.VMEM(mlp_in.shape, BF),
            pltpu.VMEM(mlp_out.shape, BF),
            pltpu.VMEM((NL * 32, CB), F32),
            pltpu.VMEM((ROWS, NL, 16, CB), BF),
            pltpu.VMEM((ROWS, NL, 16, CB), BF),
            pltpu.VMEM((NX, 2, LQ, 16, CB), BF),
            pltpu.VMEM((NX, 2, LQ, 16, CB), BF),
            pltpu.VMEM((2, NL, 16, CB), BF),
            pltpu.VMEM((4, NX, LB, 2 * CB), BF),
            pltpu.VMEM((4, NX, LB, 2 * CB), BF),
            pltpu.VMEM((2 * NX * CB, 2 * NX * CB), BF),
            pltpu.VMEM((4, NX, LB, 2 * CB), BF),
            pltpu.VMEM((4, NX, LB, 2 * CB), BF),
            pltpu.VMEM((4, NL, 16, CB), BF),
            pltpu.VMEM((4, NL, 16, CB), BF),
            pltpu.VMEM((2, NL, 16, CB), BF),
            pltpu.VMEM((2, NL, 16, CB), BF),
            pltpu.VMEM((NLON, 2 * MODES), BF),
            pltpu.VMEM((2 * NL * 16, CB), F32),
            pltpu.VMEM((CYC // 2, NX, 2 * LON, CB), BF),
            pltpu.VMEM((CYC // 2, NX, 2 * LON, CB), BF),
            pltpu.VMEM((CYC // 2, 2 * LON, NX * CB), BF),
            dma((10,)),
            dma((ROWS,)),
            dma((ROWS,)),
            dma((2,)),
            dma((2,)),
            dma((4,)),
            dma((4,)),
            dma((4,)),
            dma((4,)),
            dma((4,)),
            dma((4,)),
            dma((2,)),
            dma((2,)),
            dma((len(PIECES),)),
            dma((len(PIECES),)),
            dma((len(PIECES),)),
        ],
        compiler_params=pltpu.CompilerParams(
            collective_id=0, has_side_effects=True, vmem_limit_bytes=60 << 20
        ),
        name="sfno_block",
    )(
        m_order,
        quad_weights[None, :],
        ln_gain[None, :],
        mlp_bias[None, :],
        grid,
        jnp.asarray(table),
        jnp.asarray(np.ascontiguousarray(table.transpose(0, 2, 1))),
        legendre,
        mix_real,
        mix_imag,
        spec_gain,
        mlp_in,
        mlp_out,
    )
    out = pl.pallas_call(
        finish,
        out_shape=jax.ShapeDtypeStruct(part.shape, BF),
        in_specs=[hbm],
        out_specs=hbm,
        scratch_shapes=[
            pltpu.VMEM(part.shape, BF),
            dma((CYC // 2,)),
            dma((CYC // 2,)),
        ],
        compiler_params=pltpu.CompilerParams(vmem_limit_bytes=60 << 20),
        name="move_result",
    )(part)
    return out.reshape(CYC, LON, NX * CB)


def solution(mesh):
    placed = (P("lat", None, "ch"), P("lat", None, None)) + (P(),) * 9
    return jax.shard_map(
        body, mesh=mesh, in_specs=placed, out_specs=P("lat", "ch", None), check_vma=False
    )
```

```python
import math

import jax
import jax.numpy as jnp
import numpy as np
import ml_dtypes
from jax import lax
from jax.experimental import pallas as pl
from jax.experimental.pallas import tpu as pltpu
from jax.sharding import PartitionSpec as P

NLON = 1440
MODES = 384
NL = 64
NX = 4
CYC = 8
ROWS = 6
CB = 128
LB = MODES // NX
LQ = NL // NX
LON = NLON // NX
KP = ROWS // 2
PIECES = [(0, 0, 720), (1, 0, 720), (2, 0, 720), (3, 0, 256), (3, 256, 256), (3, 512, 208)]
MESH = pl.DeviceIdType.MESH
BF = jnp.bfloat16
F32 = jnp.float32


def twiddles():
    index = np.arange(MODES)[:, None] * np.arange(NLON)[None, :] % NLON
    angle = index * (2.0 * math.pi / NLON)
    table = np.stack([np.cos(angle), -np.sin(angle)]) / math.sqrt(NLON)
    return table.astype(np.float32).astype(ml_dtypes.bfloat16)


def dot(a, b):
    return jnp.dot(a, b, preferred_element_type=F32)


def point_layer(rows, lng, win, bias, wout):
    values = rows.astype(F32)
    center = jnp.mean(values, axis=-1, keepdims=True)
    moved = values - center
    spread = jnp.mean(moved * moved, axis=-1, keepdims=True)
    normed = (moved * lax.rsqrt(spread + 1e-05) * lng[...]).astype(BF)
    inner = dot(normed, win[...]) + bias[...]
    half = 0.5 * inner
    root = math.sqrt(2.0 / math.pi)
    bent = jnp.tanh(inner * (root + (root * 0.044715) * (inner * inner)))
    hidden = (half + half * bent).astype(BF)
    return (values + dot(hidden, wout[...])).astype(BF)


def finish(part_h, out_h, hold, i_sem, o_sem):
    pairs = range(CYC // 2)
    into = [pltpu.make_async_copy(part_h.at[p], hold.at[p], i_sem.at[p]) for p in pairs]
    out = [pltpu.make_async_copy(hold.at[p], out_h.at[p], o_sem.at[p]) for p in pairs]
    for copy in into:
        copy.start()
    for p in pairs:
        into[p].wait()
        out[p].start()
    for copy in out:
        copy.wait()


def kernel(
    morder,
    quad,
    lng,
    bias,
    grid_h,
    tw_h,
    twt_h,
    leg_h,
    mr_h,
    mi_h,
    gain_h,
    win_h,
    wout_h,
    out_h,
    grid_v,
    tw_v,
    twt_v,
    leg_v,
    legt,
    mr_v,
    mi_v,
    gain_v,
    gaind_v,
    win_v,
    wout_v,
    stage,
    sbuf,
    rbuf,
    mr_in,
    mr_out,
    sb2,
    cs,
    cr,
    wm,
    fs,
    fr,
    eq,
    rq,
    eh,
    rh,
    itab,
    xst,
    gs,
    gr,
    ov,
    load_sem,
    s_snd,
    s_rcv,
    m_snd,
    m_rcv,
    c_snd,
    c_rcv,
    f_snd,
    f_rcv,
    q_snd,
    q_rcv,
    h_snd,
    h_rcv,
    g_snd,
    g_rcv,
    o_sem,
):
    me = lax.axis_index("lat")
    x = lax.axis_index("ch")

    loads = [
        pltpu.make_async_copy(src, dst, load_sem.at[i])
        for i, (src, dst) in enumerate(
            [
                (tw_h, tw_v),
                (grid_h, grid_v),
                (mr_h, mr_v),
                (mi_h, mi_v),
                (leg_h, leg_v),
                (twt_h, twt_v),
                (gain_h.at[pl.ds(pl.multiple_of(x * LB, LB), LB)], gain_v),
                (gain_h.at[:, pl.ds(pl.multiple_of(x * CB, CB), CB)], gaind_v),
                (win_h, win_v),
                (wout_h, wout_v),
            ]
        )
    ]
    for load in loads:
        load.start()

    barrier = pltpu.get_barrier_semaphore()

    @pl.loop(1, NL)
    def _(s):
        pl.semaphore_signal(
            barrier, inc=1, device_id=(lax.rem(me + s, NL), x), device_id_type=MESH
        )

    for s in range(1, NX):
        pl.semaphore_signal(
            barrier, inc=1, device_id=(me, lax.rem(x + s, NX)), device_id_type=MESH
        )

    def lat_send(src, dst, snd, rcv):
        @pl.loop(1, NL)
        def _(s):
            j = lax.rem(me + s, NL)
            pltpu.make_async_remote_copy(
                src_ref=src.at[j],
                dst_ref=dst.at[me],
                send_sem=snd,
                recv_sem=rcv,
                device_id=(j, x),
                device_id_type=MESH,
            ).start()

        pltpu.make_async_copy(src.at[me], dst.at[me], rcv).start()

    def ch_send(src, dst, snd, rcv):
        for s in (2, 1, 3):
            i = lax.rem(x + s, NX)
            pltpu.make_async_remote_copy(
                src_ref=src(i),
                dst_ref=dst,
                send_sem=snd,
                recv_sem=rcv,
                device_id=(me, i),
                device_id_type=MESH,
            ).start()
        pltpu.make_async_copy(src(x), dst, rcv).start()

    def take(ref, sem):
        pltpu.make_async_copy(ref, ref, sem).wait()

    column = jnp.broadcast_to(morder[...].reshape(1, MODES).astype(F32), (8, MODES)).T[:, :1]
    lane = lax.broadcasted_iota(jnp.int32, (MODES, MODES), 1)
    hot = jnp.where(column.astype(jnp.int32) == lane, 1.0, 0.0).astype(BF)

    loads[0].wait()
    loads[1].wait()

    def fourier(ks):
        n = len(ks)
        at = lax.broadcasted_iota(jnp.int32, (n * NL, MODES), 0)
        at = ROWS * (at & (NL - 1)) + ks[0] + (at >> 6)
        wanted = jnp.where(at == lane[: n * NL], 1.0, 0.0).astype(BF)
        pick = dot(wanted, hot).astype(BF)
        table = jnp.concatenate(
            [dot(pick, tw_v[0]).astype(BF), dot(pick, tw_v[1]).astype(BF)], axis=0
        )
        for p in range(CYC // 2):
            res = dot(table, jnp.concatenate([grid_v[2 * p], grid_v[2 * p + 1]], axis=1))
            for reim in range(2):
                for k2 in range(n):
                    first = (reim * n + k2) * NL
                    for c in range(2):
                        row = k2 * NL * 16 + reim * 8 + 2 * p + c
                        stage[pl.ds(row, NL, stride=16), :] = res[
                            first : first + NL, c * CB : (c + 1) * CB
                        ]
        for k2 in range(n):
            part = stage[k2 * NL * 16 : (k2 + 1) * NL * 16]
            sbuf[ks[k2]] = part.astype(BF).reshape(NL, 16, CB)

    def spectra_send(src, k):
        lat_send(src, rbuf.at[k], s_snd.at[k], s_rcv.at[k])

    def split(tiles):
        tiles = tiles.astype(F32)
        n = tiles.shape[0] * 8
        return [tiles[:, i * 8 : (i + 1) * 8, :].reshape(n, CB).astype(BF) for i in range(2)]

    fourier((0,))
    pl.semaphore_wait(barrier, NL - 1 + NX - 1)
    spectra_send(sbuf.at[0], 0)

    fourier((4, 5))
    ch_send(
        lambda i: sbuf.at[pl.ds(4, 2), pl.ds(i * LQ, LQ)], mr_in.at[x], m_snd.at[0], m_rcv.at[0]
    )
    fourier((1,))
    spectra_send(sbuf.at[1], 1)
    loads[2].wait()
    loads[3].wait()
    for xs in range(NX):
        for xd in range(NX):
            re = mr_v[xs * CB : (xs + 1) * CB, xd * CB : (xd + 1) * CB]
            im = mi_v[xs * CB : (xs + 1) * CB, xd * CB : (xd + 1) * CB]
            r0, c0 = xs * 2 * CB, xd * 2 * CB
            wm[r0 : r0 + CB, c0 : c0 + CB] = re
            wm[r0 : r0 + CB, c0 + CB : c0 + 2 * CB] = im
            wm[r0 + CB : r0 + 2 * CB, c0 : c0 + CB] = -im
            wm[r0 + CB : r0 + 2 * CB, c0 + CB : c0 + 2 * CB] = re
    fourier((2, 3))
    spectra_send(sbuf.at[2], 2)
    spectra_send(sbuf.at[3], 3)

    take(mr_in, m_rcv.at[0])
    lhs = []
    for i in range(NX):
        lhs += split(mr_in[i].reshape(2 * LQ, 16, CB))
    res = dot(jnp.concatenate(lhs, axis=1), wm[...])
    for i in range(NX):
        part = [
            res[:, (2 * i + reim) * CB : (2 * i + reim + 1) * CB].reshape(2 * LQ, 8, CB)
            for reim in range(2)
        ]
        mr_out[i] = jnp.concatenate(part, axis=1).astype(BF).reshape(2, LQ, 16, CB)
    ch_send(lambda i: mr_out.at[i], sb2.at[:, pl.ds(x * LQ, LQ)], m_snd.at[1], m_rcv.at[1])

    loads[4].wait()
    for k in range(ROWS):
        values = leg_v[k]
        legt[k] = values.T
        leg_v[k] = (values.astype(F32) * quad[...]).astype(BF)
    loads[5].wait()
    order = lax.broadcasted_iota(jnp.int32, (MODES, MODES), 0)
    scale = jnp.where(order == 0, 1.0, 2.0)
    scaled = jnp.where(morder[...].reshape(1, MODES) == order, scale, 0.0).astype(BF)
    moved = jnp.where(order == ROWS * (lane & (NL - 1)) + (lane >> 6), 1.0, 0.0).astype(BF)
    scaled = dot(scaled, moved).astype(BF)
    for reim in range(2):
        itab[:, reim * MODES : (reim + 1) * MODES] = dot(twt_v[reim], scaled).astype(BF)
    loads[6].wait()
    loads[7].wait()

    sub = lax.broadcasted_iota(jnp.int32, (NL, 8, CB), 1)

    def analyse(k):
        take(rbuf.at[k], s_rcv.at[k])
        return dot(leg_v[k], jnp.concatenate(split(rbuf[k]), axis=1))

    def offer(k):
        cs[k] = analyse(k).astype(BF).reshape(NX, LB, 2 * CB)
        ch_send(lambda i: cs.at[k, i], cr.at[k, x], c_snd.at[k], c_rcv.at[k])

    def mix(k):
        take(cr.at[k], c_rcv.at[k])
        res = dot(jnp.concatenate([cr[k, i] for i in range(NX)], axis=1), wm[...])
        for i in range(NX):
            part = gain_v[:, i * CB : (i + 1) * CB]
            part = jnp.concatenate([part, part], axis=1)
            fs[k, i] = (res[:, i * 2 * CB : (i + 1) * 2 * CB] * part).astype(BF)
        ch_send(lambda i: fs.at[k, i], fr.at[k, x], f_snd.at[k], f_rcv.at[k])

    def synthesise(k, filt):
        back = dot(legt[k], filt)
        return back[:, :CB].reshape(NL, 8, CB), back[:, CB:].reshape(NL, 8, CB)

    def received(k):
        take(fr.at[k], f_rcv.at[k])
        return fr[k].reshape(MODES, 2 * CB)

    def filtered(k):
        gain = gaind_v[...]
        return (analyse(k) * jnp.concatenate([gain, gain], axis=1)).astype(BF)

    def gather(parts, first, n):
        out = None
        for i, part in enumerate(parts):
            turned = pltpu.roll(part, (n * i - first) % 8, 1)
            out = turned if out is None else jnp.where(sub < n * i, out, turned)
        return out

    def pack_quarters(backs):
        for g in range(4):
            tiles = [
                gather([*backs[2 * i], *backs[2 * i + 1]], 2 * g, 2) for i in range(2)
            ]
            eq[g] = jnp.concatenate(tiles, axis=1).astype(BF)

    def pack_half(backs, h):
        tiles = [gather(backs[i], 4 * h, 4) for i in range(2)]
        eh[h] = jnp.concatenate(tiles, axis=1).astype(BF)

    def send_quarter(g):
        lat_send(eq.at[g], rq.at[g], q_snd.at[g], q_rcv.at[g])

    def send_half(h):
        lat_send(eh.at[h], rh.at[h], h_snd.at[h], h_rcv.at[h])

    def waves(p):
        take(rq.at[p], q_rcv.at[p])
        if p % 2 == 0:
            take(rh.at[p // 2], h_rcv.at[p // 2])
        xst[: NL * 16] = rq[p].astype(F32).reshape(NL * 16, CB)
        xst[NL * 16 :] = rh[p // 2].astype(F32).reshape(NL * 16, CB)
        cols = []
        for c in range(2):
            part = []
            for reim in range(2):
                for k in range(4):
                    part.append(xst[pl.ds(k * 4 + reim * 2 + c, NL, stride=16), :])
                for k in range(2):
                    at = NL * 16 + k * 8 + reim * 4 + 2 * (p % 2) + c
                    part.append(xst[pl.ds(at, NL, stride=16), :])
            cols.append(jnp.concatenate(part, axis=0).astype(BF))
        wave = dot(itab[...], jnp.concatenate(cols, axis=1))
        both = [grid_v[2 * p + c].astype(F32) + wave[:, c * CB : (c + 1) * CB] for c in range(2)]
        for i in range(NX):
            gs[p, i] = jnp.concatenate(
                [b[i * LON : (i + 1) * LON] for b in both], axis=0
            ).astype(BF)
        for t, (pair, at, n) in enumerate(PIECES):
            if pair == p:
                part = pl.ds(at, n)
                ch_send(
                    lambda i: gs.at[p, i, part], gr.at[p, x, part], g_snd.at[t], g_rcv.at[t]
                )


    def points(t):
        p, at, n = PIECES[t]
        part = pl.ds(at, n)
        take(gr.at[p, :, part], g_rcv.at[t])
        rows = jnp.concatenate([gr[p, i, part, :] for i in range(NX)], axis=1)
        ov[p, part, :] = point_layer(rows, lng, win_v, bias, wout_v)
        copy = pltpu.make_async_copy(ov.at[p, part], out_h.at[p, part], o_sem.at[t])
        copy.start()
        return copy

    offer(0)
    take(sb2, m_rcv.at[1])
    spectra_send(sb2.at[0], 4)
    spectra_send(sb2.at[1], 5)
    offer(1)
    mix(0)
    offer(2)
    mix(1)
    backs = [synthesise(0, received(0))]
    offer(3)
    mix(2)
    backs.append(synthesise(1, received(1)))
    backs.append(synthesise(2, received(2)))
    mix(3)
    backs.append(synthesise(3, received(3)))
    pack_quarters(backs)
    send_quarter(0)
    backs = [synthesise(k, filtered(k)) for k in (4, 5)]
    pack_half(backs, 0)
    send_half(0)
    send_quarter(1)
    pack_half(backs, 1)
    send_half(1)
    send_quarter(2)
    send_quarter(3)
    loads[8].wait()
    loads[9].wait()
    waves(0)
    waves(1)
    copies = [points(0)]
    waves(2)
    waves(3)
    copies += [points(t) for t in range(1, len(PIECES))]

    for k in range(ROWS):
        take(sbuf.at[k, pl.ds(0, NL - 1)], s_snd.at[k])
    for k in range(4):
        take(cs.at[k, pl.ds(0, NX - 1)], c_snd.at[k])
        take(fs.at[k, pl.ds(0, NX - 1)], f_snd.at[k])
    for i in range(2):
        take(mr_out.at[pl.ds(0, NX - 1)], m_snd.at[i])
    for g in range(4):
        take(eq.at[g, pl.ds(0, NL - 1)], q_snd.at[g])
    for h in range(2):
        take(eh.at[h, pl.ds(0, NL - 1)], h_snd.at[h])
    for t, (p, at, n) in enumerate(PIECES):
        part = pl.ds(at, n)
        take(gs.at[p, pl.ds(0, NX - 1), part], g_snd.at[t])
    for copy in copies:
        copy.wait()


def body(
    grid,
    legendre,
    m_order,
    quad_weights,
    mix_real,
    mix_imag,
    spec_gain,
    ln_gain,
    mlp_in,
    mlp_bias,
    mlp_out,
):
    table = twiddles()
    vm = pl.BlockSpec(memory_space=pltpu.VMEM)
    hbm = pl.BlockSpec(memory_space=pl.ANY)
    dma = pltpu.SemaphoreType.DMA
    part = pl.pallas_call(
        kernel,
        out_shape=jax.ShapeDtypeStruct((CYC // 2, 2 * LON, NX * CB), BF),
        in_specs=[vm] * 4 + [hbm] * 9,
        out_specs=hbm,
        scratch_shapes=[
            pltpu.VMEM((CYC, NLON, CB), BF),
            pltpu.VMEM((2, MODES, NLON), BF),
            pltpu.VMEM((2, NLON, MODES), BF),
            pltpu.VMEM((ROWS, MODES, NL * CYC), BF),
            pltpu.VMEM((ROWS, NL * CYC, MODES), BF),
            pltpu.VMEM(mix_real.shape, BF),
            pltpu.VMEM(mix_imag.shape, BF),
            pltpu.VMEM((LB, NX * CB), F32),
            pltpu.VMEM((MODES, CB), F32),
            pltpu.VMEM(mlp_in.shape, BF),
            pltpu.VMEM(mlp_out.shape, BF),
            pltpu.VMEM((NL * 32, CB), F32),
            pltpu.VMEM((ROWS, NL, 16, CB), BF),
            pltpu.VMEM((ROWS, NL, 16, CB), BF),
            pltpu.VMEM((NX, 2, LQ, 16, CB), BF),
            pltpu.VMEM((NX, 2, LQ, 16, CB), BF),
            pltpu.VMEM((2, NL, 16, CB), BF),
            pltpu.VMEM((4, NX, LB, 2 * CB), BF),
            pltpu.VMEM((4, NX, LB, 2 * CB), BF),
            pltpu.VMEM((2 * NX * CB, 2 * NX * CB), BF),
            pltpu.VMEM((4, NX, LB, 2 * CB), BF),
            pltpu.VMEM((4, NX, LB, 2 * CB), BF),
            pltpu.VMEM((4, NL, 16, CB), BF),
            pltpu.VMEM((4, NL, 16, CB), BF),
            pltpu.VMEM((2, NL, 16, CB), BF),
            pltpu.VMEM((2, NL, 16, CB), BF),
            pltpu.VMEM((NLON, 2 * MODES), BF),
            pltpu.VMEM((2 * NL * 16, CB), F32),
            pltpu.VMEM((CYC // 2, NX, 2 * LON, CB), BF),
            pltpu.VMEM((CYC // 2, NX, 2 * LON, CB), BF),
            pltpu.VMEM((CYC // 2, 2 * LON, NX * CB), BF),
            dma((10,)),
            dma((ROWS,)),
            dma((ROWS,)),
            dma((2,)),
            dma((2,)),
            dma((4,)),
            dma((4,)),
            dma((4,)),
            dma((4,)),
            dma((4,)),
            dma((4,)),
            dma((2,)),
            dma((2,)),
            dma((len(PIECES),)),
            dma((len(PIECES),)),
            dma((len(PIECES),)),
        ],
        compiler_params=pltpu.CompilerParams(
            collective_id=0, has_side_effects=True, vmem_limit_bytes=60 << 20
        ),
        name="sfno_block",
    )(
        m_order,
        quad_weights[None, :],
        ln_gain[None, :],
        mlp_bias[None, :],
        grid,
        jnp.asarray(table),
        jnp.asarray(np.ascontiguousarray(table.transpose(0, 2, 1))),
        legendre,
        mix_real,
        mix_imag,
        spec_gain,
        mlp_in,
        mlp_out,
    )
    out = pl.pallas_call(
        finish,
        out_shape=jax.ShapeDtypeStruct(part.shape, BF),
        in_specs=[hbm],
        out_specs=hbm,
        scratch_shapes=[
            pltpu.VMEM(part.shape, BF),
            dma((CYC // 2,)),
            dma((CYC // 2,)),
        ],
        compiler_params=pltpu.CompilerParams(vmem_limit_bytes=60 << 20),
        name="move_result",
    )(part)
    return out.reshape(CYC, LON, NX * CB)


def solution(mesh):
    placed = (P("lat", None, "ch"), P("lat", None, None)) + (P(),) * 9
    return jax.shard_map(
        body, mesh=mesh, in_specs=placed, out_specs=P("lat", "ch", None), check_vma=False
    )
```

```python
import math

import jax
import jax.numpy as jnp
import numpy as np
import ml_dtypes
from jax import lax
from jax.experimental import pallas as pl
from jax.experimental.pallas import tpu as pltpu
from jax.sharding import PartitionSpec as P

NLON = 1440
MODES = 384
NL = 64
NX = 4
CYC = 8
ROWS = 6
CB = 128
LB = MODES // NX
LQ = NL // NX
LON = NLON // NX
KP = ROWS // 2
PIECES = [(0, 0, 720), (1, 0, 720), (2, 0, 720), (3, 0, 256), (3, 256, 256), (3, 512, 208)]
MESH = pl.DeviceIdType.MESH
BF = jnp.bfloat16
F32 = jnp.float32


def twiddles():
    index = np.arange(MODES)[:, None] * np.arange(NLON)[None, :] % NLON
    angle = index * (2.0 * math.pi / NLON)
    table = np.stack([np.cos(angle), -np.sin(angle)]) / math.sqrt(NLON)
    return table.astype(np.float32).astype(ml_dtypes.bfloat16)


def dot(a, b):
    return jnp.dot(a, b, preferred_element_type=F32)


def point_layer(rows, lng, win, bias, wout):
    values = rows.astype(F32)
    center = jnp.mean(values, axis=-1, keepdims=True)
    moved = values - center
    spread = jnp.mean(moved * moved, axis=-1, keepdims=True)
    normed = (moved * lax.rsqrt(spread + 1e-05) * lng[...]).astype(BF)
    inner = dot(normed, win[...]) + bias[...]
    half = 0.5 * inner
    root = math.sqrt(2.0 / math.pi)
    bent = jnp.tanh(inner * (root + (root * 0.044715) * (inner * inner)))
    hidden = (half + half * bent).astype(BF)
    return (values + dot(hidden, wout[...])).astype(BF)


def finish(part_h, out_h, hold, i_sem, o_sem):
    pairs = range(CYC // 2)
    into = [pltpu.make_async_copy(part_h.at[p], hold.at[p], i_sem.at[p]) for p in pairs]
    out = [pltpu.make_async_copy(hold.at[p], out_h.at[p], o_sem.at[p]) for p in pairs]
    for copy in into:
        copy.start()
    for p in pairs:
        into[p].wait()
        out[p].start()
    for copy in out:
        copy.wait()


def kernel(
    morder,
    quad,
    lng,
    bias,
    grid_h,
    tw_h,
    twt_h,
    leg_h,
    mr_h,
    mi_h,
    gain_h,
    win_h,
    wout_h,
    out_h,
    grid_v,
    tw_v,
    twt_v,
    leg_v,
    legt,
    mr_v,
    mi_v,
    gain_v,
    gaind_v,
    win_v,
    wout_v,
    stage,
    sbuf,
    rbuf,
    mr_in,
    mr_out,
    sb2,
    cs,
    cr,
    wm,
    fs,
    fr,
    eq,
    rq,
    eh,
    rh,
    itab,
    xst,
    gs,
    gr,
    ov,
    load_sem,
    s_snd,
    s_rcv,
    m_snd,
    m_rcv,
    c_snd,
    c_rcv,
    f_snd,
    f_rcv,
    q_snd,
    q_rcv,
    h_snd,
    h_rcv,
    g_snd,
    g_rcv,
    o_sem,
):
    me = lax.axis_index("lat")
    x = lax.axis_index("ch")

    loads = [
        pltpu.make_async_copy(src, dst, load_sem.at[i])
        for i, (src, dst) in enumerate(
            [
                (tw_h, tw_v),
                (grid_h, grid_v),
                (mr_h, mr_v),
                (mi_h, mi_v),
                (leg_h, leg_v),
                (twt_h, twt_v),
                (gain_h.at[pl.ds(pl.multiple_of(x * LB, LB), LB)], gain_v),
                (gain_h.at[:, pl.ds(pl.multiple_of(x * CB, CB), CB)], gaind_v),
                (win_h, win_v),
                (wout_h, wout_v),
            ]
        )
    ]
    for load in loads:
        load.start()

    barrier = pltpu.get_barrier_semaphore()

    @pl.loop(1, NL)
    def _(s):
        pl.semaphore_signal(
            barrier, inc=1, device_id=(lax.rem(me + s, NL), x), device_id_type=MESH
        )

    for s in range(1, NX):
        pl.semaphore_signal(
            barrier, inc=1, device_id=(me, lax.rem(x + s, NX)), device_id_type=MESH
        )

    def lat_send(src, dst, snd, rcv):
        @pl.loop(1, NL)
        def _(s):
            j = lax.rem(me + s, NL)
            pltpu.make_async_remote_copy(
                src_ref=src.at[j],
                dst_ref=dst.at[me],
                send_sem=snd,
                recv_sem=rcv,
                device_id=(j, x),
                device_id_type=MESH,
            ).start()

        pltpu.make_async_copy(src.at[me], dst.at[me], rcv).start()

    def ch_send(src, dst, snd, rcv):
        for s in (2, 1, 3):
            i = lax.rem(x + s, NX)
            pltpu.make_async_remote_copy(
                src_ref=src(i),
                dst_ref=dst,
                send_sem=snd,
                recv_sem=rcv,
                device_id=(me, i),
                device_id_type=MESH,
            ).start()
        pltpu.make_async_copy(src(x), dst, rcv).start()

    def take(ref, sem):
        pltpu.make_async_copy(ref, ref, sem).wait()

    order = lax.broadcasted_iota(jnp.int32, (MODES, MODES), 0)
    place = lax.broadcasted_iota(jnp.int32, (MODES, MODES), 1)
    moved = jnp.where(order == ROWS * (place % NL) + place // NL, 1.0, 0.0).astype(BF)
    hot = dot(jnp.where(morder[...].reshape(1, MODES) == order, 1.0, 0.0).astype(BF), moved)
    pick = hot.T.astype(BF)

    loads[0].wait()
    loads[1].wait()

    def fourier(kp):
        rows = pick[kp * 2 * NL : (kp + 1) * 2 * NL]
        table = jnp.concatenate(
            [dot(rows, tw_v[0]).astype(BF), dot(rows, tw_v[1]).astype(BF)], axis=0
        )
        for p in range(CYC // 2):
            res = dot(table, jnp.concatenate([grid_v[2 * p], grid_v[2 * p + 1]], axis=1))
            for reim in range(2):
                for k2 in range(2):
                    at = (reim * 2 + k2) * NL
                    for c in range(2):
                        row = k2 * NL * 16 + reim * 8 + 2 * p + c
                        stage[pl.ds(row, NL, stride=16), :] = res[
                            at : at + NL, c * CB : (c + 1) * CB
                        ]
        for k2 in range(2):
            part = stage[k2 * NL * 16 : (k2 + 1) * NL * 16]
            sbuf[2 * kp + k2] = part.astype(BF).reshape(NL, 16, CB)

    def spectra_send(src, k):
        lat_send(src, rbuf.at[k], s_snd.at[k], s_rcv.at[k])

    def split(tiles):
        tiles = tiles.astype(F32)
        n = tiles.shape[0] * 8
        return [tiles[:, i * 8 : (i + 1) * 8, :].reshape(n, CB).astype(BF) for i in range(2)]

    fourier(0)
    pl.semaphore_wait(barrier, NL - 1 + NX - 1)
    spectra_send(sbuf.at[0], 0)

    fourier(2)
    ch_send(
        lambda i: sbuf.at[pl.ds(4, 2), pl.ds(i * LQ, LQ)], mr_in.at[x], m_snd.at[0], m_rcv.at[0]
    )
    spectra_send(sbuf.at[1], 1)
    loads[2].wait()
    loads[3].wait()
    for xs in range(NX):
        for xd in range(NX):
            re = mr_v[xs * CB : (xs + 1) * CB, xd * CB : (xd + 1) * CB]
            im = mi_v[xs * CB : (xs + 1) * CB, xd * CB : (xd + 1) * CB]
            r0, c0 = xs * 2 * CB, xd * 2 * CB
            wm[r0 : r0 + CB, c0 : c0 + CB] = re
            wm[r0 : r0 + CB, c0 + CB : c0 + 2 * CB] = im
            wm[r0 + CB : r0 + 2 * CB, c0 : c0 + CB] = -im
            wm[r0 + CB : r0 + 2 * CB, c0 + CB : c0 + 2 * CB] = re
    fourier(1)
    spectra_send(sbuf.at[2], 2)
    spectra_send(sbuf.at[3], 3)

    take(mr_in, m_rcv.at[0])
    lhs = []
    for i in range(NX):
        lhs += split(mr_in[i].reshape(2 * LQ, 16, CB))
    res = dot(jnp.concatenate(lhs, axis=1), wm[...])
    for i in range(NX):
        part = [
            res[:, (2 * i + reim) * CB : (2 * i + reim + 1) * CB].reshape(2 * LQ, 8, CB)
            for reim in range(2)
        ]
        mr_out[i] = jnp.concatenate(part, axis=1).astype(BF).reshape(2, LQ, 16, CB)
    ch_send(lambda i: mr_out.at[i], sb2.at[:, pl.ds(x * LQ, LQ)], m_snd.at[1], m_rcv.at[1])

    loads[4].wait()
    for k in range(ROWS):
        values = leg_v[k]
        legt[k] = values.T
        leg_v[k] = (values.astype(F32) * quad[...]).astype(BF)
    loads[5].wait()
    hot = (hot * jnp.where(order == 0, 1.0, 2.0)).astype(BF)
    for reim in range(2):
        itab[:, reim * MODES : (reim + 1) * MODES] = dot(twt_v[reim], hot).astype(BF)
    loads[6].wait()
    loads[7].wait()

    sub = lax.broadcasted_iota(jnp.int32, (NL, 8, CB), 1)

    def analyse(k):
        take(rbuf.at[k], s_rcv.at[k])
        return dot(leg_v[k], jnp.concatenate(split(rbuf[k]), axis=1))

    def offer(k):
        cs[k] = analyse(k).astype(BF).reshape(NX, LB, 2 * CB)
        ch_send(lambda i: cs.at[k, i], cr.at[k, x], c_snd.at[k], c_rcv.at[k])

    def mix(k):
        take(cr.at[k], c_rcv.at[k])
        res = dot(jnp.concatenate([cr[k, i] for i in range(NX)], axis=1), wm[...])
        for i in range(NX):
            part = gain_v[:, i * CB : (i + 1) * CB]
            part = jnp.concatenate([part, part], axis=1)
            fs[k, i] = (res[:, i * 2 * CB : (i + 1) * 2 * CB] * part).astype(BF)
        ch_send(lambda i: fs.at[k, i], fr.at[k, x], f_snd.at[k], f_rcv.at[k])

    def synthesise(k, filt):
        back = dot(legt[k], filt)
        return back[:, :CB].reshape(NL, 8, CB), back[:, CB:].reshape(NL, 8, CB)

    def received(k):
        take(fr.at[k], f_rcv.at[k])
        return fr[k].reshape(MODES, 2 * CB)

    def filtered(k):
        gain = gaind_v[...]
        return (analyse(k) * jnp.concatenate([gain, gain], axis=1)).astype(BF)

    def gather(parts, first, n):
        out = None
        for i, part in enumerate(parts):
            turned = pltpu.roll(part, (n * i - first) % 8, 1)
            out = turned if out is None else jnp.where(sub < n * i, out, turned)
        return out

    def pack_quarters(backs):
        for g in range(4):
            tiles = [
                gather([*backs[2 * i], *backs[2 * i + 1]], 2 * g, 2) for i in range(2)
            ]
            eq[g] = jnp.concatenate(tiles, axis=1).astype(BF)

    def pack_halves(backs):
        for h in range(2):
            tiles = [gather(backs[i], 4 * h, 4) for i in range(2)]
            eh[h] = jnp.concatenate(tiles, axis=1).astype(BF)

    def send_quarter(g):
        lat_send(eq.at[g], rq.at[g], q_snd.at[g], q_rcv.at[g])

    def send_half(h):
        lat_send(eh.at[h], rh.at[h], h_snd.at[h], h_rcv.at[h])

    def waves(p):
        take(rq.at[p], q_rcv.at[p])
        if p % 2 == 0:
            take(rh.at[p // 2], h_rcv.at[p // 2])
        xst[: NL * 16] = rq[p].astype(F32).reshape(NL * 16, CB)
        xst[NL * 16 :] = rh[p // 2].astype(F32).reshape(NL * 16, CB)
        cols = []
        for c in range(2):
            part = []
            for reim in range(2):
                for k in range(4):
                    part.append(xst[pl.ds(k * 4 + reim * 2 + c, NL, stride=16), :])
                for k in range(2):
                    at = NL * 16 + k * 8 + reim * 4 + 2 * (p % 2) + c
                    part.append(xst[pl.ds(at, NL, stride=16), :])
            cols.append(jnp.concatenate(part, axis=0).astype(BF))
        wave = dot(itab[...], jnp.concatenate(cols, axis=1))
        both = [grid_v[2 * p + c].astype(F32) + wave[:, c * CB : (c + 1) * CB] for c in range(2)]
        for i in range(NX):
            gs[p, i] = jnp.concatenate(
                [b[i * LON : (i + 1) * LON] for b in both], axis=0
            ).astype(BF)
        send_piece(p)

    def send_piece(t):
        p, at, n = PIECES[t]
        part = pl.ds(at, n)
        ch_send(lambda i: gs.at[p, i, part], gr.at[p, x, part], g_snd.at[t], g_rcv.at[t])

    def points(t, follow=None):
        p, at, n = PIECES[t]
        part = pl.ds(at, n)
        take(gr.at[p, :, part], g_rcv.at[t])
        if follow is not None:
            send_piece(follow)
        rows = jnp.concatenate([gr[p, i, part, :] for i in range(NX)], axis=1)
        ov[p, part, :] = point_layer(rows, lng, win_v, bias, wout_v)
        copy = pltpu.make_async_copy(ov.at[p, part], out_h.at[p, part], o_sem.at[t])
        copy.start()
        return copy

    offer(0)
    take(sb2, m_rcv.at[1])
    spectra_send(sb2.at[0], 4)
    spectra_send(sb2.at[1], 5)
    offer(1)
    mix(0)
    offer(2)
    mix(1)
    backs = [synthesise(0, received(0))]
    offer(3)
    mix(2)
    backs.append(synthesise(1, received(1)))
    backs.append(synthesise(2, received(2)))
    mix(3)
    backs.append(synthesise(3, received(3)))
    pack_quarters(backs)
    send_quarter(0)
    pack_halves([synthesise(k, filtered(k)) for k in (4, 5)])
    send_half(0)
    send_quarter(1)
    send_half(1)
    send_quarter(2)
    send_quarter(3)
    loads[8].wait()
    loads[9].wait()
    waves(0)
    waves(1)
    copies = [points(0)]
    waves(2)
    waves(3)
    copies.append(points(1))
    send_piece(4)
    copies.append(points(2, 5))
    copies += [points(t) for t in range(3, len(PIECES))]

    for k in range(ROWS):
        take(sbuf.at[k, pl.ds(0, NL - 1)], s_snd.at[k])
    for k in range(4):
        take(cs.at[k, pl.ds(0, NX - 1)], c_snd.at[k])
        take(fs.at[k, pl.ds(0, NX - 1)], f_snd.at[k])
    for i in range(2):
        take(mr_out.at[pl.ds(0, NX - 1)], m_snd.at[i])
    for g in range(4):
        take(eq.at[g, pl.ds(0, NL - 1)], q_snd.at[g])
    for h in range(2):
        take(eh.at[h, pl.ds(0, NL - 1)], h_snd.at[h])
    for t, (p, at, n) in enumerate(PIECES):
        part = pl.ds(at, n)
        take(gs.at[p, pl.ds(0, NX - 1), part], g_snd.at[t])
    for copy in copies:
        copy.wait()


def body(
    grid,
    legendre,
    m_order,
    quad_weights,
    mix_real,
    mix_imag,
    spec_gain,
    ln_gain,
    mlp_in,
    mlp_bias,
    mlp_out,
):
    table = twiddles()
    vm = pl.BlockSpec(memory_space=pltpu.VMEM)
    hbm = pl.BlockSpec(memory_space=pl.ANY)
    dma = pltpu.SemaphoreType.DMA
    part = pl.pallas_call(
        kernel,
        out_shape=jax.ShapeDtypeStruct((CYC // 2, 2 * LON, NX * CB), BF),
        in_specs=[vm] * 4 + [hbm] * 9,
        out_specs=hbm,
        scratch_shapes=[
            pltpu.VMEM((CYC, NLON, CB), BF),
            pltpu.VMEM((2, MODES, NLON), BF),
            pltpu.VMEM((2, NLON, MODES), BF),
            pltpu.VMEM((ROWS, MODES, NL * CYC), BF),
            pltpu.VMEM((ROWS, NL * CYC, MODES), BF),
            pltpu.VMEM(mix_real.shape, BF),
            pltpu.VMEM(mix_imag.shape, BF),
            pltpu.VMEM((LB, NX * CB), F32),
            pltpu.VMEM((MODES, CB), F32),
            pltpu.VMEM(mlp_in.shape, BF),
            pltpu.VMEM(mlp_out.shape, BF),
            pltpu.VMEM((NL * 32, CB), F32),
            pltpu.VMEM((ROWS, NL, 16, CB), BF),
            pltpu.VMEM((ROWS, NL, 16, CB), BF),
            pltpu.VMEM((NX, 2, LQ, 16, CB), BF),
            pltpu.VMEM((NX, 2, LQ, 16, CB), BF),
            pltpu.VMEM((2, NL, 16, CB), BF),
            pltpu.VMEM((4, NX, LB, 2 * CB), BF),
            pltpu.VMEM((4, NX, LB, 2 * CB), BF),
            pltpu.VMEM((2 * NX * CB, 2 * NX * CB), BF),
            pltpu.VMEM((4, NX, LB, 2 * CB), BF),
            pltpu.VMEM((4, NX, LB, 2 * CB), BF),
            pltpu.VMEM((4, NL, 16, CB), BF),
            pltpu.VMEM((4, NL, 16, CB), BF),
            pltpu.VMEM((2, NL, 16, CB), BF),
            pltpu.VMEM((2, NL, 16, CB), BF),
            pltpu.VMEM((NLON, 2 * MODES), BF),
            pltpu.VMEM((2 * NL * 16, CB), F32),
            pltpu.VMEM((CYC // 2, NX, 2 * LON, CB), BF),
            pltpu.VMEM((CYC // 2, NX, 2 * LON, CB), BF),
            pltpu.VMEM((CYC // 2, 2 * LON, NX * CB), BF),
            dma((10,)),
            dma((ROWS,)),
            dma((ROWS,)),
            dma((2,)),
            dma((2,)),
            dma((4,)),
            dma((4,)),
            dma((4,)),
            dma((4,)),
            dma((4,)),
            dma((4,)),
            dma((2,)),
            dma((2,)),
            dma((len(PIECES),)),
            dma((len(PIECES),)),
            dma((len(PIECES),)),
        ],
        compiler_params=pltpu.CompilerParams(
            collective_id=0, has_side_effects=True, vmem_limit_bytes=60 << 20
        ),
        name="sfno_block",
    )(
        m_order,
        quad_weights[None, :],
        ln_gain[None, :],
        mlp_bias[None, :],
        grid,
        jnp.asarray(table),
        jnp.asarray(np.ascontiguousarray(table.transpose(0, 2, 1))),
        legendre,
        mix_real,
        mix_imag,
        spec_gain,
        mlp_in,
        mlp_out,
    )
    out = pl.pallas_call(
        finish,
        out_shape=jax.ShapeDtypeStruct(part.shape, BF),
        in_specs=[hbm],
        out_specs=hbm,
        scratch_shapes=[
            pltpu.VMEM(part.shape, BF),
            dma((CYC // 2,)),
            dma((CYC // 2,)),
        ],
        compiler_params=pltpu.CompilerParams(vmem_limit_bytes=60 << 20),
        name="move_result",
    )(part)
    return out.reshape(CYC, LON, NX * CB)


def solution(mesh):
    placed = (P("lat", None, "ch"), P("lat", None, None)) + (P(),) * 9
    return jax.shard_map(
        body, mesh=mesh, in_specs=placed, out_specs=P("lat", "ch", None), check_vma=False
    )
```

```python
import math

import jax
import jax.numpy as jnp
import numpy as np
import ml_dtypes
from jax import lax
from jax.experimental import pallas as pl
from jax.experimental.pallas import tpu as pltpu
from jax.sharding import PartitionSpec as P

NLON = 1440
MODES = 384
NL = 64
NX = 4
CYC = 8
ROWS = 6
CB = 128
LB = MODES // NX
LQ = NL // NX
LON = NLON // NX
KP = ROWS // 2
PIECES = [(0, 0, 720), (1, 0, 720), (2, 0, 720), (3, 0, 240), (3, 240, 240), (3, 480, 240)]
MESH = pl.DeviceIdType.MESH
BF = jnp.bfloat16
F32 = jnp.float32


def twiddles():
    index = np.arange(MODES)[:, None] * np.arange(NLON)[None, :] % NLON
    angle = index * (2.0 * math.pi / NLON)
    table = np.stack([np.cos(angle), -np.sin(angle)]) / math.sqrt(NLON)
    return table.astype(np.float32).astype(ml_dtypes.bfloat16)


def dot(a, b):
    return jnp.dot(a, b, preferred_element_type=F32)


def point_layer(rows, lng, win, bias, wout):
    values = rows.astype(F32)
    center = jnp.mean(values, axis=-1, keepdims=True)
    moved = values - center
    spread = jnp.mean(moved * moved, axis=-1, keepdims=True)
    normed = (moved * lax.rsqrt(spread + 1e-05) * lng[...]).astype(BF)
    inner = dot(normed, win[...]) + bias[...]
    half = 0.5 * inner
    root = math.sqrt(2.0 / math.pi)
    bent = jnp.tanh(inner * (root + (root * 0.044715) * (inner * inner)))
    hidden = (half + half * bent).astype(BF)
    return (values + dot(hidden, wout[...])).astype(BF)


def finish(part_h, out_h, hold, i_sem, o_sem):
    pairs = range(CYC // 2)
    into = [pltpu.make_async_copy(part_h.at[p], hold.at[p], i_sem.at[p]) for p in pairs]
    out = [pltpu.make_async_copy(hold.at[p], out_h.at[p], o_sem.at[p]) for p in pairs]
    for copy in into:
        copy.start()
    for p in pairs:
        into[p].wait()
        out[p].start()
    for copy in out:
        copy.wait()


def kernel(
    morder,
    quad,
    lng,
    bias,
    grid_h,
    tw_h,
    twt_h,
    leg_h,
    mr_h,
    mi_h,
    gain_h,
    win_h,
    wout_h,
    out_h,
    grid_v,
    tw_v,
    twt_v,
    leg_v,
    legt,
    mr_v,
    mi_v,
    gain_v,
    gaind_v,
    win_v,
    wout_v,
    stage,
    sbuf,
    rbuf,
    mr_in,
    mr_out,
    sb2,
    cs,
    cr,
    wm,
    fs,
    fr,
    eq,
    rq,
    eh,
    rh,
    itab,
    xst,
    gs,
    gr,
    ov,
    load_sem,
    s_snd,
    s_rcv,
    m_snd,
    m_rcv,
    c_snd,
    c_rcv,
    f_snd,
    f_rcv,
    q_snd,
    q_rcv,
    h_snd,
    h_rcv,
    g_snd,
    g_rcv,
    o_sem,
):
    me = lax.axis_index("lat")
    x = lax.axis_index("ch")

    loads = [
        pltpu.make_async_copy(src, dst, load_sem.at[i])
        for i, (src, dst) in enumerate(
            [
                (tw_h, tw_v),
                (grid_h, grid_v),
                (mr_h, mr_v),
                (mi_h, mi_v),
                (leg_h, leg_v),
                (twt_h, twt_v),
                (gain_h.at[pl.ds(pl.multiple_of(x * LB, LB), LB)], gain_v),
                (gain_h.at[:, pl.ds(pl.multiple_of(x * CB, CB), CB)], gaind_v),
                (win_h, win_v),
                (wout_h, wout_v),
            ]
        )
    ]
    for load in loads:
        load.start()

    barrier = pltpu.get_barrier_semaphore()

    @pl.loop(1, NL)
    def _(s):
        pl.semaphore_signal(
            barrier, inc=1, device_id=(lax.rem(me + s, NL), x), device_id_type=MESH
        )

    for s in range(1, NX):
        pl.semaphore_signal(
            barrier, inc=1, device_id=(me, lax.rem(x + s, NX)), device_id_type=MESH
        )

    def lat_send(src, dst, snd, rcv):
        @pl.loop(1, NL)
        def _(s):
            j = lax.rem(me + s, NL)
            pltpu.make_async_remote_copy(
                src_ref=src.at[j],
                dst_ref=dst.at[me],
                send_sem=snd,
                recv_sem=rcv,
                device_id=(j, x),
                device_id_type=MESH,
            ).start()

        pltpu.make_async_copy(src.at[me], dst.at[me], rcv).start()

    def ch_send(src, dst, snd, rcv):
        for s in (2, 1, 3):
            i = lax.rem(x + s, NX)
            pltpu.make_async_remote_copy(
                src_ref=src(i),
                dst_ref=dst,
                send_sem=snd,
                recv_sem=rcv,
                device_id=(me, i),
                device_id_type=MESH,
            ).start()
        pltpu.make_async_copy(src(x), dst, rcv).start()

    def take(ref, sem):
        pltpu.make_async_copy(ref, ref, sem).wait()

    order = lax.broadcasted_iota(jnp.int32, (MODES, MODES), 0)
    place = lax.broadcasted_iota(jnp.int32, (MODES, MODES), 1)
    moved = jnp.where(order == ROWS * (place % NL) + place // NL, 1.0, 0.0).astype(BF)
    hot = dot(jnp.where(morder[...].reshape(1, MODES) == order, 1.0, 0.0).astype(BF), moved)
    pick = hot.T.astype(BF)

    loads[0].wait()
    loads[1].wait()

    def fourier(kp):
        rows = pick[kp * 2 * NL : (kp + 1) * 2 * NL]
        table = jnp.concatenate(
            [dot(rows, tw_v[0]).astype(BF), dot(rows, tw_v[1]).astype(BF)], axis=0
        )
        @pl.loop(0, CYC // 2)
        def _(p):
            res = dot(table, jnp.concatenate([grid_v[2 * p], grid_v[2 * p + 1]], axis=1))
            for reim in range(2):
                for k2 in range(2):
                    at = (reim * 2 + k2) * NL
                    for c in range(2):
                        row = k2 * NL * 16 + reim * 8 + 2 * p + c
                        stage[pl.ds(row, NL, stride=16), :] = res[
                            at : at + NL, c * CB : (c + 1) * CB
                        ]

        for k2 in range(2):
            part = stage[k2 * NL * 16 : (k2 + 1) * NL * 16]
            sbuf[2 * kp + k2] = part.astype(BF).reshape(NL, 16, CB)

    def spectra_send(src, k):
        lat_send(src, rbuf.at[k], s_snd.at[k], s_rcv.at[k])

    def split(tiles):
        tiles = tiles.astype(F32)
        n = tiles.shape[0] * 8
        return [tiles[:, i * 8 : (i + 1) * 8, :].reshape(n, CB).astype(BF) for i in range(2)]

    fourier(0)
    pl.semaphore_wait(barrier, NL - 1 + NX - 1)
    spectra_send(sbuf.at[0], 0)

    fourier(2)
    ch_send(
        lambda i: sbuf.at[pl.ds(4, 2), pl.ds(i * LQ, LQ)], mr_in.at[x], m_snd.at[0], m_rcv.at[0]
    )
    spectra_send(sbuf.at[1], 1)
    loads[2].wait()
    loads[3].wait()
    for xs in range(NX):
        for xd in range(NX):
            re = mr_v[xs * CB : (xs + 1) * CB, xd * CB : (xd + 1) * CB]
            im = mi_v[xs * CB : (xs + 1) * CB, xd * CB : (xd + 1) * CB]
            r0, c0 = xs * 2 * CB, xd * 2 * CB
            wm[r0 : r0 + CB, c0 : c0 + CB] = re
            wm[r0 : r0 + CB, c0 + CB : c0 + 2 * CB] = im
            wm[r0 + CB : r0 + 2 * CB, c0 : c0 + CB] = -im
            wm[r0 + CB : r0 + 2 * CB, c0 + CB : c0 + 2 * CB] = re
    fourier(1)
    spectra_send(sbuf.at[2], 2)
    spectra_send(sbuf.at[3], 3)

    take(mr_in, m_rcv.at[0])
    lhs = []
    for i in range(NX):
        lhs += split(mr_in[i].reshape(2 * LQ, 16, CB))
    res = dot(jnp.concatenate(lhs, axis=1), wm[...])
    for i in range(NX):
        part = [
            res[:, (2 * i + reim) * CB : (2 * i + reim + 1) * CB].reshape(2 * LQ, 8, CB)
            for reim in range(2)
        ]
        mr_out[i] = jnp.concatenate(part, axis=1).astype(BF).reshape(2, LQ, 16, CB)
    ch_send(lambda i: mr_out.at[i], sb2.at[:, pl.ds(x * LQ, LQ)], m_snd.at[1], m_rcv.at[1])

    loads[4].wait()
    for k in range(ROWS):
        values = leg_v[k]
        legt[k] = values.T
        leg_v[k] = (values.astype(F32) * quad[...]).astype(BF)
    loads[5].wait()
    hot = (hot * jnp.where(order == 0, 1.0, 2.0)).astype(BF)
    for reim in range(2):
        itab[:, reim * MODES : (reim + 1) * MODES] = dot(twt_v[reim], hot).astype(BF)
    loads[6].wait()
    loads[7].wait()

    sub = lax.broadcasted_iota(jnp.int32, (NL, 8, CB), 1)

    def analyse(k):
        take(rbuf.at[k], s_rcv.at[k])
        return dot(leg_v[k], jnp.concatenate(split(rbuf[k]), axis=1))

    def offer(k):
        cs[k] = analyse(k).astype(BF).reshape(NX, LB, 2 * CB)
        ch_send(lambda i: cs.at[k, i], cr.at[k, x], c_snd.at[k], c_rcv.at[k])

    def mix(k):
        take(cr.at[k], c_rcv.at[k])
        res = dot(jnp.concatenate([cr[k, i] for i in range(NX)], axis=1), wm[...])
        for i in range(NX):
            part = gain_v[:, i * CB : (i + 1) * CB]
            part = jnp.concatenate([part, part], axis=1)
            fs[k, i] = (res[:, i * 2 * CB : (i + 1) * 2 * CB] * part).astype(BF)
        ch_send(lambda i: fs.at[k, i], fr.at[k, x], f_snd.at[k], f_rcv.at[k])

    def synthesise(k, filt):
        back = dot(legt[k], filt)
        return back[:, :CB].reshape(NL, 8, CB), back[:, CB:].reshape(NL, 8, CB)

    def received(k):
        take(fr.at[k], f_rcv.at[k])
        return fr[k].reshape(MODES, 2 * CB)

    def filtered(k):
        gain = gaind_v[...]
        return (analyse(k) * jnp.concatenate([gain, gain], axis=1)).astype(BF)

    def gather(parts, first, n):
        out = None
        for i, part in enumerate(parts):
            turned = pltpu.roll(part, (n * i - first) % 8, 1)
            out = turned if out is None else jnp.where(sub < n * i, out, turned)
        return out

    def pack_quarters(backs):
        for g in range(4):
            tiles = [
                gather([*backs[2 * i], *backs[2 * i + 1]], 2 * g, 2) for i in range(2)
            ]
            eq[g] = jnp.concatenate(tiles, axis=1).astype(BF)

    def pack_halves(backs):
        for h in range(2):
            tiles = [gather(backs[i], 4 * h, 4) for i in range(2)]
            eh[h] = jnp.concatenate(tiles, axis=1).astype(BF)

    def send_quarter(g):
        lat_send(eq.at[g], rq.at[g], q_snd.at[g], q_rcv.at[g])

    def send_half(h):
        lat_send(eh.at[h], rh.at[h], h_snd.at[h], h_rcv.at[h])

    def waves(p):
        take(rq.at[p], q_rcv.at[p])
        if p % 2 == 0:
            take(rh.at[p // 2], h_rcv.at[p // 2])
        xst[: NL * 16] = rq[p].astype(F32).reshape(NL * 16, CB)
        xst[NL * 16 :] = rh[p // 2].astype(F32).reshape(NL * 16, CB)
        cols = []
        for c in range(2):
            part = []
            for reim in range(2):
                for k in range(4):
                    part.append(xst[pl.ds(k * 4 + reim * 2 + c, NL, stride=16), :])
                for k in range(2):
                    at = NL * 16 + k * 8 + reim * 4 + 2 * (p % 2) + c
                    part.append(xst[pl.ds(at, NL, stride=16), :])
            cols.append(jnp.concatenate(part, axis=0).astype(BF))
        wave = dot(itab[...], jnp.concatenate(cols, axis=1))
        both = [grid_v[2 * p + c].astype(F32) + wave[:, c * CB : (c + 1) * CB] for c in range(2)]
        for i in range(NX):
            gs[p, i] = jnp.concatenate(
                [b[i * LON : (i + 1) * LON] for b in both], axis=0
            ).astype(BF)
        send_piece(p)

    def send_piece(t):
        p, at, n = PIECES[t]
        part = pl.ds(at, n)
        ch_send(lambda i: gs.at[p, i, part], gr.at[p, x, part], g_snd.at[t], g_rcv.at[t])

    def points(t, follow=None):
        p, at, n = PIECES[t]
        part = pl.ds(at, n)
        take(gr.at[p, :, part], g_rcv.at[t])
        if follow is not None:
            send_piece(follow)

        @pl.loop(0, n // 240)
        def _(b):
            block = pl.ds(pl.multiple_of(at + b * 240, 16), 240)
            rows = jnp.concatenate([gr[p, i, block, :] for i in range(NX)], axis=1)
            ov[p, block, :] = point_layer(rows, lng, win_v, bias, wout_v)

        copy = pltpu.make_async_copy(ov.at[p, part], out_h.at[p, part], o_sem.at[t])
        copy.start()
        return copy

    offer(0)
    take(sb2, m_rcv.at[1])
    spectra_send(sb2.at[0], 4)
    spectra_send(sb2.at[1], 5)
    offer(1)
    mix(0)
    offer(2)
    mix(1)
    backs = [synthesise(0, received(0))]
    offer(3)
    mix(2)
    backs.append(synthesise(1, received(1)))
    backs.append(synthesise(2, received(2)))
    mix(3)
    backs.append(synthesise(3, received(3)))
    pack_quarters(backs)
    send_quarter(0)
    pack_halves([synthesise(k, filtered(k)) for k in (4, 5)])
    send_half(0)
    send_quarter(1)
    send_half(1)
    send_quarter(2)
    send_quarter(3)
    loads[8].wait()
    loads[9].wait()
    waves(0)
    waves(1)
    copies = [points(0)]
    waves(2)
    waves(3)
    copies.append(points(1))
    send_piece(4)
    copies.append(points(2, 5))
    copies += [points(t) for t in range(3, len(PIECES))]

    for k in range(ROWS):
        take(sbuf.at[k, pl.ds(0, NL - 1)], s_snd.at[k])
    for k in range(4):
        take(cs.at[k, pl.ds(0, NX - 1)], c_snd.at[k])
        take(fs.at[k, pl.ds(0, NX - 1)], f_snd.at[k])
    for i in range(2):
        take(mr_out.at[pl.ds(0, NX - 1)], m_snd.at[i])
    for g in range(4):
        take(eq.at[g, pl.ds(0, NL - 1)], q_snd.at[g])
    for h in range(2):
        take(eh.at[h, pl.ds(0, NL - 1)], h_snd.at[h])
    for t, (p, at, n) in enumerate(PIECES):
        part = pl.ds(at, n)
        take(gs.at[p, pl.ds(0, NX - 1), part], g_snd.at[t])
    for copy in copies:
        copy.wait()


def body(
    grid,
    legendre,
    m_order,
    quad_weights,
    mix_real,
    mix_imag,
    spec_gain,
    ln_gain,
    mlp_in,
    mlp_bias,
    mlp_out,
):
    table = twiddles()
    vm = pl.BlockSpec(memory_space=pltpu.VMEM)
    hbm = pl.BlockSpec(memory_space=pl.ANY)
    dma = pltpu.SemaphoreType.DMA
    part = pl.pallas_call(
        kernel,
        out_shape=jax.ShapeDtypeStruct((CYC // 2, 2 * LON, NX * CB), BF),
        in_specs=[vm] * 4 + [hbm] * 9,
        out_specs=hbm,
        scratch_shapes=[
            pltpu.VMEM((CYC, NLON, CB), BF),
            pltpu.VMEM((2, MODES, NLON), BF),
            pltpu.VMEM((2, NLON, MODES), BF),
            pltpu.VMEM((ROWS, MODES, NL * CYC), BF),
            pltpu.VMEM((ROWS, NL * CYC, MODES), BF),
            pltpu.VMEM(mix_real.shape, BF),
            pltpu.VMEM(mix_imag.shape, BF),
            pltpu.VMEM((LB, NX * CB), F32),
            pltpu.VMEM((MODES, CB), F32),
            pltpu.VMEM(mlp_in.shape, BF),
            pltpu.VMEM(mlp_out.shape, BF),
            pltpu.VMEM((NL * 32, CB), F32),
            pltpu.VMEM((ROWS, NL, 16, CB), BF),
            pltpu.VMEM((ROWS, NL, 16, CB), BF),
            pltpu.VMEM((NX, 2, LQ, 16, CB), BF),
            pltpu.VMEM((NX, 2, LQ, 16, CB), BF),
            pltpu.VMEM((2, NL, 16, CB), BF),
            pltpu.VMEM((4, NX, LB, 2 * CB), BF),
            pltpu.VMEM((4, NX, LB, 2 * CB), BF),
            pltpu.VMEM((2 * NX * CB, 2 * NX * CB), BF),
            pltpu.VMEM((4, NX, LB, 2 * CB), BF),
            pltpu.VMEM((4, NX, LB, 2 * CB), BF),
            pltpu.VMEM((4, NL, 16, CB), BF),
            pltpu.VMEM((4, NL, 16, CB), BF),
            pltpu.VMEM((2, NL, 16, CB), BF),
            pltpu.VMEM((2, NL, 16, CB), BF),
            pltpu.VMEM((NLON, 2 * MODES), BF),
            pltpu.VMEM((2 * NL * 16, CB), F32),
            pltpu.VMEM((CYC // 2, NX, 2 * LON, CB), BF),
            pltpu.VMEM((CYC // 2, NX, 2 * LON, CB), BF),
            pltpu.VMEM((CYC // 2, 2 * LON, NX * CB), BF),
            dma((10,)),
            dma((ROWS,)),
            dma((ROWS,)),
            dma((2,)),
            dma((2,)),
            dma((4,)),
            dma((4,)),
            dma((4,)),
            dma((4,)),
            dma((4,)),
            dma((4,)),
            dma((2,)),
            dma((2,)),
            dma((len(PIECES),)),
            dma((len(PIECES),)),
            dma((len(PIECES),)),
        ],
        compiler_params=pltpu.CompilerParams(
            collective_id=0, has_side_effects=True, vmem_limit_bytes=60 << 20
        ),
        name="sfno_block",
    )(
        m_order,
        quad_weights[None, :],
        ln_gain[None, :],
        mlp_bias[None, :],
        grid,
        jnp.asarray(table),
        jnp.asarray(np.ascontiguousarray(table.transpose(0, 2, 1))),
        legendre,
        mix_real,
        mix_imag,
        spec_gain,
        mlp_in,
        mlp_out,
    )
    out = pl.pallas_call(
        finish,
        out_shape=jax.ShapeDtypeStruct(part.shape, BF),
        in_specs=[hbm],
        out_specs=hbm,
        scratch_shapes=[
            pltpu.VMEM(part.shape, BF),
            dma((CYC // 2,)),
            dma((CYC // 2,)),
        ],
        compiler_params=pltpu.CompilerParams(vmem_limit_bytes=60 << 20),
        name="move_result",
    )(part)
    return out.reshape(CYC, LON, NX * CB)


def solution(mesh):
    placed = (P("lat", None, "ch"), P("lat", None, None)) + (P(),) * 9
    return jax.shard_map(
        body, mesh=mesh, in_specs=placed, out_specs=P("lat", "ch", None), check_vma=False
    )
```
